128 devices in a mesh: seq: 32 (over x, y, z_hi), sp: 4 (over z_lo, core).
Axes of the slice: x: 4, y: 4, z: 4 (z_hi: 2, z_lo: 2; z = z_hi * 2 + z_lo), core: 2. Of those that a mesh axis runs over, the one named last changes fastest.
Arguments:
- group_hidden: bfloat16 [384, 5120], P('seq', 'sp'), may hold values from -30 to 30
- queries: bfloat16 [384, 5120], P('seq', 'sp'), may hold values from -18 to 18
- history_keys: bfloat16 [65536, 5120], P('seq', 'sp'), may hold values from -6 to 6
- history_values: bfloat16 [65536, 5120], P('seq', 'sp'), may hold values from -16 to 16
- valid_len: int32 [32], P('seq'), may hold values from 512 to 2048, as said below
- out_weight: bfloat16 [5120, 5120], P('sp', 'seq'), may hold values from -0.078125 to 0.078125
- attn_gate: float32 [5120], P('sp'), may hold values from 0.5 to 1.5
- head_gain: float32 [5120], replicated, may hold values from 0.25 to 1.75
- head_shift: float32 [5120], replicated, may hold values from -6 to 6
- head_weight: float32 [5120, 64], replicated, may hold values from -0.078125 to 0.078125
- head_bias: float32 [64], replicated, may hold values from -6 to 6
- noisy_latent: float32 [64, 24, 16], P('seq', 'sp'), may hold values from -6 to 6
- prev_latent: bfloat16 [2, 64, 24, 16], P(None, 'seq', 'sp'), may hold values from -6 to 6
- prev_feat: bfloat16 [2, 64, 24, 384], P(None, 'seq', 'sp'), may hold values from -6 to 6
- conv_in_weight: bfloat16 [3, 3, 3, 16, 384], replicated, may hold values from -0.3125 to 0.3125
- conv_in_bias: float32 [384], replicated, may hold values from -6 to 6
- vae_gain: float32 [384], replicated, may hold values from 0.25 to 1.75
- conv_mid_weight: bfloat16 [3, 3, 3, 384, 384], replicated, may hold values from -0.0625 to 0.0625
- conv_mid_bias: float32 [384], replicated, may hold values from -6 to 6
Outputs:
- hidden_out: bfloat16 [384, 5120], P('seq', 'sp')
- decoded: float32 [64, 24, 384], P('seq', 'sp')
The draws below stay inside these ranges and needn't reach their ends.
Inputs may be any that keep to these rules, and one draw needn't show every extreme that they name: `valid_len`: every block has at least 512 visible positions; some block is fully visible.
All inputs are finite; a program needn't handle non-finite values.
Results may differ from the reference program's by a relative error of at most 0.0085.
Values may be sent and summed in bfloat16 or wider, within the bound.
A program may use at most 320 MiB of HBM per device.

```python
import math
import jax
import jax.numpy as jnp
from jax import lax

D = 5120
HEADS = 40
HD = 128
C_LAT = 16
C_VAE = 384
PW = 12
L_DEV = 2048
PH = 32
Q_TOK = 384
HIST = 65536
LH = 64
LW = 24
N_SEQ = 32


def draw_queries(key, part):
    key = jax.random.fold_in(key, 5)
    values = jnp.clip(3.0 * jax.random.normal(key, (Q_TOK, D), jnp.float32), -18.0, 18.0)
    return values.astype(jnp.bfloat16)


def draw_history_keys(key, part):
    key = jax.random.fold_in(key, 6)
    values = jnp.clip(jax.random.normal(key, (HIST, D), jnp.float32), -6.0, 6.0)
    return values.astype(jnp.bfloat16)


def draw_valid_len(key, part):
    key = jax.random.fold_in(key, 7)
    block_count = HIST // L_DEV
    lengths = jax.random.randint(key, (block_count,), L_DEV // 4, L_DEV + 1)
    full_block = jax.random.randint(jax.random.fold_in(key, 1), (), 0, block_count)
    return jnp.where(jnp.arange(block_count) == full_block, L_DEV, lengths).astype(jnp.int32)


def draw_group_hidden(key, part):
    key = jax.random.fold_in(key, 11)
    key_base, key_row, key_col = jax.random.split(key, 3)
    base = jnp.clip(jax.random.normal(key_base, (Q_TOK, D), jnp.float32), -6.0, 6.0)
    row_scale = jnp.exp(jax.random.uniform(key_row, (Q_TOK, 1), jnp.float32, 0.0, 2.302585))
    rising = jnp.exp(1.098612 * jnp.arange(D, dtype=jnp.float32) / D)[None, :]
    col_scale = rising * jnp.exp(jax.random.uniform(key_col, (1, D), jnp.float32, 0.0, 1.203973))
    return (base * row_scale * col_scale / 20.0).astype(jnp.bfloat16)


def steps_of(own_key, shape, cuts, least, largest):
    def one(dim, blocks):
        draws = jax.random.uniform(jax.random.fold_in(jax.random.fold_in(own_key, 6), dim), (blocks,), jnp.float32, least / len(cuts), largest / len(cuts))
        return jnp.repeat(jnp.exp(draws), shape[dim] // blocks).reshape((-1,) + (1,) * (len(shape) - dim - 1))

    gain = one(*cuts[0])
    for cut in cuts[1:]:
        gain = gain * one(*cut)
    return gain


def noise(rng, shape, scale, bound, shards=(), kind=jnp.bfloat16):
    values = jax.random.normal(rng, shape, jnp.float32) * scale
    if len(shards) > 0:
        values = steps_of(rng, shape, shards, -0.22, 0.18) * values
    return jnp.clip(values, min=-bound, max=bound).astype(kind)


def setup_inputs(seed: int = 0) -> dict:
    splits = jax.random.split(jax.random.key(seed), 20)
    group_hidden = draw_group_hidden(jax.random.fold_in(splits[19], 71), 0)
    queries = draw_queries(jax.random.fold_in(splits[19], 71), 0)
    history_keys = draw_history_keys(jax.random.fold_in(splits[19], 71), 0)
    history_values = noise(splits[3], (HIST, D), 3.0, 16.0, ((0, 32), (1, 4)))
    valid_len = draw_valid_len(jax.random.fold_in(splits[19], 71), 0)
    out_weight = noise(splits[5], (D, D), D ** -0.5, 0.078125, ((0, 4), (1, 32)))
    attn_gate = jnp.clip(0.5 + 1.0 * jax.random.uniform(splits[6], (D,), jnp.float32) ** steps_of(splits[6], (D,), ((0, 4),), -0.2, 0.2), 0.5, 1.5)
    head_gain = jnp.clip(1.0 + 0.15 * jax.random.normal(splits[7], (D,), jnp.float32), 0.25, 1.75)
    head_shift = noise(splits[8], (D,), 0.5, 6.0, (), jnp.float32)
    head_weight = noise(splits[9], (D, 4 * C_LAT), D ** -0.5, 0.078125, (), jnp.float32)
    head_bias = noise(splits[10], (4 * C_LAT,), 0.5, 6.0, (), jnp.float32)
    noisy_latent = noise(splits[11], (LH, LW, C_LAT), 1.0, 6.0, ((0, 32), (1, 4)), jnp.float32)
    prev_latent = noise(splits[12], (2, LH, LW, C_LAT), 1.0, 6.0, ((1, 32), (2, 4)))
    prev_feat = noise(splits[13], (2, LH, LW, C_VAE), 1.0, 6.0, ((1, 32), (2, 4)))
    conv_in_weight = noise(splits[14], (3, 3, 3, C_LAT, C_VAE), (27 * C_LAT) ** -0.5, 0.3125)
    conv_in_bias = noise(splits[15], (C_VAE,), 0.5, 6.0, (), jnp.float32)
    vae_gain = jnp.clip(1.0 + 0.15 * jax.random.normal(splits[16], (C_VAE,), jnp.float32), 0.25, 1.75)
    conv_mid_weight = noise(splits[17], (3, 3, 3, C_VAE, C_VAE), (27 * C_VAE) ** -0.5, 0.0625)
    conv_mid_bias = noise(splits[18], (C_VAE,), 0.5, 6.0, (), jnp.float32)
    return {"group_hidden": group_hidden, "queries": queries, "history_keys": history_keys, "history_values": history_values, "valid_len": valid_len, "out_weight": out_weight, "attn_gate": attn_gate, "head_gain": head_gain, "head_shift": head_shift, "head_weight": head_weight, "head_bias": head_bias, "noisy_latent": noisy_latent, "prev_latent": prev_latent, "prev_feat": prev_feat, "conv_in_weight": conv_in_weight, "conv_in_bias": conv_in_bias, "vae_gain": vae_gain, "conv_mid_weight": conv_mid_weight, "conv_mid_bias": conv_mid_bias}


noise_level = 0.75

def causal_conv(earlier, current, weight, bias):
    frames = jnp.concatenate([earlier, current[None]], axis=0)
    padded = jnp.pad(frames, ((0, 0), (1, 1), (1, 1), (0, 0)))
    row_count, col_count = (current.shape[0], current.shape[1])
    tap_list = [padded[step_t, shift_h:shift_h + row_count, shift_w:shift_w + col_count, :] for step_t in range(3) for shift_h in range(3) for shift_w in range(3)]
    columns = jnp.concatenate(tap_list, axis=-1).reshape(row_count * col_count, -1)
    result = jnp.dot(columns, weight.reshape(-1, weight.shape[-1]), preferred_element_type=jnp.float32) + bias
    return result.reshape(row_count, col_count, -1)

def reference(group_hidden, queries, history_keys, history_values, valid_len, out_weight, attn_gate, head_gain, head_shift, head_weight, head_bias, noisy_latent, prev_latent, prev_feat, conv_in_weight, conv_in_bias, vae_gain, conv_mid_weight, conv_mid_bias):
    scale = 1.0 / math.sqrt(HD)
    query_f = queries.astype(jnp.float32).reshape(Q_TOK, HEADS, HD)

    def block_step(state_now, block_id):
        best, total, accum = state_now
        row_start = (block_id * L_DEV).astype(jnp.int32)
        keys_f = lax.dynamic_slice_in_dim(history_keys, row_start, L_DEV, 0).astype(jnp.float32).reshape(L_DEV, HEADS, HD)
        values_f = lax.dynamic_slice_in_dim(history_values, row_start, L_DEV, 0).astype(jnp.float32).reshape(L_DEV, HEADS, HD)
        scores = jnp.einsum('qhd,khd->qhk', query_f, keys_f) * scale
        visible = (jnp.arange(L_DEV, dtype=jnp.int32) < valid_len[block_id])[None, None, :]
        scores = jnp.where(visible, scores, -1e+30)
        block_max = lax.optimization_barrier(jnp.max(scores, axis=-1))
        weights = jnp.where(visible, jnp.exp(scores - block_max[..., None]), 0.0).astype(jnp.bfloat16)
        weights_f = weights.astype(jnp.float32)
        block_sum = lax.optimization_barrier(jnp.sum(weights_f, axis=-1))
        block_acc = jnp.einsum('qhk,khd->qhd', weights_f, values_f)
        new_best = jnp.maximum(best, block_max)
        old_scale = jnp.exp(best - new_best)
        new_scale = jnp.exp(block_max - new_best)
        total = total * old_scale + block_sum * new_scale
        accum = accum * old_scale[..., None] + block_acc * new_scale[..., None]
        return ((new_best, total, accum), None)
    start_state = (jnp.full((Q_TOK, HEADS), -1e+30, jnp.float32), jnp.zeros((Q_TOK, HEADS), jnp.float32), jnp.zeros((Q_TOK, HEADS, HD), jnp.float32))
    (best, total, accum), _ = lax.scan(block_step, start_state, jnp.arange(N_SEQ, dtype=jnp.int32))
    attention = (accum / total[..., None]).reshape(Q_TOK, D).astype(jnp.bfloat16)
    projected = jnp.dot(attention, out_weight, preferred_element_type=jnp.float32)
    updated = group_hidden.astype(jnp.float32) + attn_gate * projected
    hidden_out = updated.astype(jnp.bfloat16)
    mean_val = lax.optimization_barrier(jnp.sum(updated, axis=-1, keepdims=True)) / D
    var_val = lax.optimization_barrier(jnp.sum(updated * updated, axis=-1, keepdims=True)) / D - mean_val * mean_val
    normed = (updated - mean_val) * lax.rsqrt(var_val + 1e-06) * head_gain + head_shift
    velocity = jnp.dot(normed, head_weight, precision=lax.Precision.HIGHEST, preferred_element_type=jnp.float32) + head_bias
    velocity = velocity.reshape(PH, PW, 2, 2, C_LAT).transpose(0, 2, 1, 3, 4).reshape(LH, LW, C_LAT)
    clean = (noisy_latent - noise_level * velocity).astype(jnp.bfloat16)
    first = causal_conv(prev_latent, clean, conv_in_weight, conv_in_bias)
    norm_scale = lax.rsqrt(lax.optimization_barrier(jnp.mean(first * first, axis=-1, keepdims=True)) + 1e-06)
    activated = jax.nn.silu(first * norm_scale * vae_gain).astype(jnp.bfloat16)
    decoded = first + causal_conv(prev_feat, activated, conv_mid_weight, conv_mid_bias)
    return (hidden_out, decoded)
```

```python
import functools
import math

import jax
import jax.numpy as jnp
from jax import lax
from jax.experimental import pallas as pl
from jax.experimental.pallas import tpu as pltpu
from jax.sharding import PartitionSpec as P

MESH = pl.DeviceIdType.MESH
BF16 = jnp.bfloat16
F32 = jnp.float32

D = 5120
HD = 128
NSEQ = 32
NSP = 4
TOK = 12
PAD = 16
TOKENS = NSEQ * TOK
HIST = 2048
FEAT = 1280
COLS = 160
CH = 5
CW = FEAT // CH
VAE = 384
EXP2_SCALE = math.log2(math.e) / math.sqrt(HD)
NOISE = 0.75


def iota(shape, dim):
    return lax.broadcasted_iota(jnp.int32, shape, dim)


def wait_bytes(region, sem):
    pltpu.make_async_copy(region, region, sem).wait()


def pad_rows(rows):
    width = rows.shape[-1]
    pairs = rows.reshape(-1, 2 * TOK, width)
    even = pairs[:, :PAD]
    odd = pltpu.roll(pairs, TOK, 1)[:, :PAD]
    return jnp.concatenate([even[:, None], odd[:, None]], axis=1).reshape(-1, PAD, width)


def pack_rows(blocks):
    width = blocks.shape[-1]
    pairs = blocks.reshape(-1, 2, PAD, width)
    zeros = jnp.zeros((pairs.shape[0], 8, width), F32)
    even = jnp.concatenate([pairs[:, 0], zeros], axis=1)
    odd = pltpu.roll(jnp.concatenate([pairs[:, 1], zeros], axis=1), TOK, 1)
    row = iota(even.shape, 1)
    return jnp.where(row < TOK, even, odd).reshape(-1, width)


def kernel(
    hidden_ref,
    q_ref,
    k_hbm,
    v_hbm,
    valid_ref,
    w_hbm,
    rows_ref,
    vecs_ref,
    bias_ref,
    headw_hbm,
    noisy_ref,
    platent_ref,
    pfeat_ref,
    win_hbm,
    wmid_hbm,
    hidden_out,
    decoded_out,
    k_s,
    v_s,
    w_s,
    headw_s,
    win_s,
    wmid_s,
    qs,
    qg,
    pc,
    rc,
    ao,
    ag,
    es,
    er,
    gs,
    gr,
    ls,
    lr,
    fs,
    fr,
    fpad,
    cells,
    vtok,
    vcell,
    feats,
    firsts,
    acts,
    proj,
    upd,
    ksem,
    vsem,
    wsem,
    lsem,
    q_send,
    q_recv,
    c_send,
    c_recv,
    d_send,
    d_recv,
    e_send,
    e_recv,
    g_send,
    g_recv,
    l_send,
    l_recv,
    f_send,
    f_recv,
):
    s = lax.axis_index("seq")
    p = lax.axis_index("sp")
    owner_sp = s // 8
    piece = lax.rem(s, 8)

    barrier = pltpu.get_barrier_semaphore()

    def greet(to_s, to_p):
        pl.semaphore_signal(barrier, inc=1, device_id=(to_s, to_p), device_id_type=MESH)

    def greet_seq(k, _):
        greet(lax.rem(s + k, NSEQ), p)
        return 0

    lax.fori_loop(1, NSEQ, greet_seq, 0)

    def greet_sources(k, _):
        greet(p * 8 + k // 3, lax.rem(p + 1 + lax.rem(k, 3), NSP))
        return 0

    lax.fori_loop(0, 24, greet_sources, 0)
    for ds in (-1, 0, 1):

        @pl.when(jnp.logical_and(s + ds >= 0, s + ds < NSEQ))
        def _():
            for dp in (1, 2, 3):
                greet(s + ds, lax.rem(p + dp, NSP))

    loads = []
    for c in range(CH):
        cols = pl.ds(c * CW, CW)
        kc = pltpu.make_async_copy(k_hbm.at[:, cols], k_s.at[c], ksem.at[c])
        vc = pltpu.make_async_copy(v_hbm.at[:, cols], v_s.at[c], vsem.at[c])
        kc.start()
        vc.start()
        loads.append((kc, vc))
    w_copy = pltpu.make_async_copy(w_hbm, w_s, wsem.at[0])
    head_rows = pl.ds(pl.multiple_of(p * FEAT, FEAT), FEAT)
    head_copy = pltpu.make_async_copy(headw_hbm.at[head_rows], headw_s, wsem.at[1])
    win_copy = pltpu.make_async_copy(win_hbm, win_s, wsem.at[2])
    wmid_copy = pltpu.make_async_copy(wmid_hbm, wmid_s, wsem.at[3])
    for copy in (win_copy, wmid_copy, w_copy, head_copy):
        copy.start()

    qs[...] = jnp.zeros(qs.shape, BF16)
    for c in range(CH):
        qs[c, 0:TOK, :] = q_ref[:, c * CW : (c + 1) * CW]
    q_own = pltpu.make_async_copy(qs, qg.at[:, s], lsem.at[0])
    q_own.start()

    ls[...] = jnp.zeros(ls.shape, F32)
    ls[:, 0:6, 0:16] = noisy_ref[...]
    ls[:, 0:6, 16:32] = platent_ref[0].astype(F32)
    ls[:, 0:6, 32:48] = platent_ref[1].astype(F32)
    fpad[...] = jnp.zeros(fpad.shape, F32)
    fpad[:, 0:6, :] = pfeat_ref[...].reshape(4, 6, VAE).astype(F32)
    fs[...] = fpad[...].reshape(32, VAE).astype(BF16)

    rows_in = 1 + jnp.where(s > 0, 1, 0) + jnp.where(s < NSEQ - 1, 1, 0)
    pl.semaphore_wait(barrier, NSEQ - 1 + jnp.where(owner_sp != p, NSEQ, 0) + 3 * rows_in)

    def send_chunk(buf, dst, c, send_sem, recv_sem, by_dest):
        def one(k, _):
            to = lax.rem(s + k, NSEQ)
            pltpu.make_async_remote_copy(
                src_ref=buf.at[c, to] if by_dest else buf.at[c],
                dst_ref=dst.at[c, s],
                send_sem=send_sem.at[c],
                recv_sem=recv_sem.at[c],
                device_id=(to, p),
                device_id_type=MESH,
            ).start()
            return 0

        lax.fori_loop(1, NSEQ, one, 0)

    for c in range(CH):
        send_chunk(qs, qg, c, q_send, q_recv, False)

    def near(fn):
        for ds in (-1, 0, 1):
            for dp in (-1, 0, 1):
                if ds == 0 and dp == 0:
                    continue
                inside_s = jnp.logical_and(s + ds >= 0, s + ds < NSEQ)
                inside_p = jnp.logical_and(p + dp >= 0, p + dp < NSP)
                pl.when(jnp.logical_and(inside_s, inside_p))(functools.partial(fn, ds, dp))

    def slot_of(ds, dp):
        return (ds + 1) * 3 + dp + 1

    def border_copies(ds, dp):
        out, back = slot_of(ds, dp), slot_of(-ds, -dp)
        return [
            pltpu.make_async_remote_copy(
                src_ref=src,
                dst_ref=dst.at[back],
                send_sem=send.at[out],
                recv_sem=recv.at[back],
                device_id=(s + ds, p + dp),
                device_id_type=MESH,
            )
            for src, dst, send, recv in ((ls, lr, l_send, l_recv), (fs, fr, f_send, f_recv))
        ]

    def border_start(ds, dp):
        for copy in border_copies(ds, dp):
            copy.start()

    def border_wait(ds, dp):
        slot = slot_of(ds, dp)
        wait_bytes(lr.at[slot], l_recv.at[slot])
        wait_bytes(fr.at[slot], f_recv.at[slot])
        wait_bytes(lr.at[slot], l_send.at[slot])
        wait_bytes(fr.at[slot], f_send.at[slot])

    near(border_start)

    visible = iota((1, HIST), 1) < valid_ref[0]
    ones = jnp.ones((HIST, HD), BF16)
    half = TOKENS // 2
    lane = iota((half, HD), 1) % 32
    q_own.wait()
    for c in range(CH):
        wait_bytes(qg.at[c, 0 : NSEQ - 1], q_recv.at[c])
        loads[c][0].wait()
        loads[c][1].wait()
        for r in range(2):
            first_owner = r * (NSEQ // 2)
            block = qg[c, first_owner : first_owner + NSEQ // 2]
            q = pack_rows(block.astype(F32)).astype(BF16)
            stats = jnp.zeros((half, HD), F32)
            for h in range(2):
                cols = slice(h * HD, (h + 1) * HD)
                scores = lax.dot_general(
                    q[:, cols],
                    k_s[c, :, cols],
                    (((1,), (1,)), ((), ())),
                    preferred_element_type=F32,
                )
                scores = jnp.where(visible, scores, -1e30)
                top = jnp.max(scores, axis=1, keepdims=True) * EXP2_SCALE
                top = top.astype(BF16).astype(F32)
                weights = jnp.exp2(scores * EXP2_SCALE - top).astype(BF16)
                both = jnp.concatenate([v_s[c, :, cols], ones], axis=1)
                acc = jnp.dot(weights, both, preferred_element_type=F32)
                total = acc[:, HD:]
                high = total.astype(BF16).astype(F32)
                stats = jnp.where(lane == h, top, stats)
                stats = jnp.where(lane == 2 + h, high, stats)
                stats = jnp.where(lane == 4 + h, total - high, stats)
                padded = pad_rows(acc[:, :HD])
                if h == 1:
                    st = pad_rows(stats)
                    at = iota(st.shape, 2)
                    spare = jnp.where(
                        at < 32,
                        pltpu.roll(st, 12, 1),
                        jnp.where(at < 64, pltpu.roll(st, 8, 1), pltpu.roll(st, 4, 1)),
                    )
                    padded = jnp.where(iota(st.shape, 1) < TOK, padded, spare)
                pc[c, first_owner : first_owner + NSEQ // 2, :, cols] = padded.astype(BF16)
        own = pltpu.make_async_copy(pc.at[c, s], rc.at[c, s], lsem.at[1 + c])
        own.start()
        send_chunk(pc, rc, c, c_send, c_recv, True)

    near(border_wait)
    win_copy.wait()
    wmid_copy.wait()
    lr[4] = ls[...]
    fr[4] = fs[...]
    cells[...] = jnp.zeros(cells.shape, F32)
    feats[...] = jnp.zeros(feats.shape, F32)
    for ds in (-1, 0, 1):
        for dp in (-1, 0, 1):
            inside = jnp.logical_and(
                jnp.logical_and(s + ds >= 0, s + ds < NSEQ),
                jnp.logical_and(p + dp >= 0, p + dp < NSP),
            )
            slot = slot_of(ds, dp)
            src = {-1: slice(4, 6), 0: slice(0, 6), 1: slice(0, 2)}[dp]
            dst = {-1: slice(0, 2), 0: slice(2, 8), 1: slice(8, 10)}[dp]
            for g in range(3):
                part = lr[slot, :, src, g * 16 : (g + 1) * 16]
                cells[g, 2 * ds + 2 : 2 * ds + 4, dst, :] = jnp.where(inside, part, 0.0)
            src = {-1: slice(5, 6), 0: slice(0, 6), 1: slice(0, 1)}[dp]
            dst = {-1: slice(0, 1), 0: slice(1, 7), 1: slice(7, 8)}[dp]
            part = fr[slot].astype(F32).reshape(2, 2, 8, VAE)
            part = jnp.where(inside, part, 0.0)
            rows = {-1: (1,), 0: (0, 1), 1: (0,)}[ds]
            for row in rows:
                for f in range(2):
                    feats[f, {-1: 0, 0: 1 + row, 1: 3}[ds], dst, :] = part[f, row, src, :]

    def window(ref, g, dy, dx, height):
        return ref[g, dy : dy + height, dx : dx + 8, :].reshape(height * 8, -1).astype(BF16)

    def taps():
        return [(dy, dx) for dy in range(3) for dx in range(3)]

    first = jnp.zeros((32, VAE), F32) + bias_ref[0:1, :]
    mid = jnp.zeros((16, VAE), F32) + bias_ref[2:3, :]
    for f in range(2):
        for dy, dx in taps():
            tap = f * 9 + dy * 3 + dx
            first += jnp.dot(window(cells, f + 1, dy, dx, 4), win_s[tap], preferred_element_type=F32)
            mid += jnp.dot(window(feats, f, dy, dx, 2), wmid_s[tap], preferred_element_type=F32)
    firsts[:, 0:8, :] = first.reshape(4, 8, VAE)

    row = iota((PAD, HD), 0)
    for c in range(CH):
        pltpu.make_async_copy(pc.at[c, s], rc.at[c, s], lsem.at[1 + c]).wait()
        wait_bytes(rc.at[c, 0 : NSEQ - 1], c_recv.at[c])
        tile = rc[c, :, :, HD : 2 * HD].astype(F32)
        at = iota(tile.shape, 1)
        st = jnp.where(
            at < 4,
            pltpu.roll(tile, 4, 1),
            jnp.where(
                at < 8,
                pltpu.roll(pltpu.roll(tile, HD - 32, 2), 8, 1),
                pltpu.roll(pltpu.roll(tile, HD - 64, 2), 12, 1),
            ),
        )
        top = jnp.max(st, axis=0, keepdims=True)
        factor = jnp.exp2(st - top)
        sums = pltpu.roll(st, HD - 2, 2) + pltpu.roll(st, HD - 4, 2)
        total = jnp.sum(factor * sums, axis=0, keepdims=True)
        factor = factor / total
        for h in range(2):
            part = rc[c, :, :, h * HD : (h + 1) * HD].astype(F32)
            merged = jnp.sum(part * factor[:, :, h : h + 1], axis=0)
            merged = jnp.where(row < TOK, merged, 0.0)
            ao[c, :, h * HD : (h + 1) * HD] = merged.astype(BF16)
        own = pltpu.make_async_copy(ao.at[c], ag.at[c, s], lsem.at[1 + CH + c])
        own.start()
        send_chunk(ao, ag, c, d_send, d_recv, False)

    w_copy.wait()
    result = jnp.zeros((NSEQ * PAD, COLS), F32)
    for c in range(CH):
        pltpu.make_async_copy(ao.at[c], ag.at[c, s], lsem.at[1 + CH + c]).wait()
        wait_bytes(ag.at[c, 0 : NSEQ - 1], d_recv.at[c])
        block = ag[c].reshape(NSEQ * PAD, CW)
        result += jnp.dot(block, w_s[c * CW : (c + 1) * CW, :], preferred_element_type=F32)
    es[:, :, 0:COLS] = result.reshape(NSEQ, PAD, COLS).astype(BF16)
    es[:, :, COLS:] = jnp.zeros((NSEQ, PAD, 256 - COLS), BF16)
    e_slot = piece * NSP + p
    same = owner_sp == p

    def send_piece(k, _):
        to = lax.rem(s + k, NSEQ)
        pltpu.make_async_remote_copy(
            src_ref=es.at[to],
            dst_ref=er.at[e_slot],
            send_sem=e_send,
            recv_sem=e_recv,
            device_id=(to, owner_sp),
            device_id_type=MESH,
        ).start()
        return 0

    lax.fori_loop(1, NSEQ, send_piece, 0)

    @pl.when(same)
    def _():
        own = pltpu.make_async_copy(es.at[s], er.at[e_slot], lsem.at[1 + 2 * CH])
        own.start()
        own.wait()
        wait_bytes(er.at[0 : NSEQ - 1], e_recv)

    @pl.when(jnp.logical_not(same))
    def _():
        send_piece(0, 0)
        wait_bytes(er, e_recv)

    for j in range(8):
        part = er[j * NSP : (j + 1) * NSP].astype(F32)
        proj[:, j * COLS : (j + 1) * COLS] = jnp.sum(part, axis=0)[:, 0:COLS]
    upd[...] = jnp.zeros(upd.shape, F32)
    upd[0:TOK, :] = hidden_ref[...].astype(F32)
    updated = upd[...] + rows_ref[0:1, :] * proj[...]
    hidden_out[...] = updated[0:TOK].astype(BF16)
    gain, shift = rows_ref[1:2, :], rows_ref[2:3, :]
    at = iota((PAD, FEAT), 0)
    left = jnp.where(at < TOK, updated * gain, jnp.where(at == TOK, gain, shift))
    head_copy.wait()
    part = jnp.dot(
        left, headw_s[...], precision=lax.Precision.HIGHEST, preferred_element_type=F32
    )
    gs[...] = jnp.zeros(gs.shape, F32)
    gs[:, 0:64] = part
    gs[:, 64:65] = jnp.sum(updated, axis=1, keepdims=True)
    gs[:, 65:66] = jnp.sum(updated * updated, axis=1, keepdims=True)

    def share(fn):
        for ds in (-1, 0, 1):
            for dp in range(NSP):
                if ds == 0 and dp == 0:
                    continue
                inside = jnp.logical_and(s + ds >= 0, s + ds < NSEQ)
                pl.when(inside)(functools.partial(fn, ds, dp))

    def g_start(ds, dp):
        pltpu.make_async_remote_copy(
            src_ref=gs,
            dst_ref=gr.at[(1 - ds) * NSP + dp],
            send_sem=g_send.at[(ds + 1) * NSP + dp],
            recv_sem=g_recv.at[(1 - ds) * NSP + dp],
            device_id=(s + ds, lax.rem(p + dp, NSP)),
            device_id_type=MESH,
        ).start()

    def g_wait(ds, dp):
        slot = (ds + 1) * NSP + dp
        wait_bytes(gr.at[slot], g_recv.at[slot])
        wait_bytes(gr.at[slot], g_send.at[slot])

    share(g_start)
    gr[NSP] = gs[...]
    share(g_wait)

    vtok[...] = jnp.zeros(vtok.shape, F32)
    vcell[...] = jnp.zeros(vcell.shape, F32)
    for ds in (-1, 0, 1):
        inside = jnp.logical_and(s + ds >= 0, s + ds < NSEQ)
        total = gr[(ds + 1) * NSP]
        for dp in range(1, NSP):
            total = total + gr[(ds + 1) * NSP + dp]
        mean = total[0:TOK, 64:65] / D
        var = total[0:TOK, 65:66] / D - mean * mean
        scaled = (total[0:TOK, 0:64] - mean * total[12:13, 0:64]) * lax.rsqrt(var + 1e-6)
        velocity = scaled + total[13:14, 0:64] + vecs_ref[0:1, 0:64]
        vtok[ds + 1, 1 : TOK + 1, 0:64] = jnp.where(inside, velocity, 0.0)
        around = vtok[ds + 1, pl.ds(3 * p, 8), :]
        for a in range(2):
            for c2 in range(2):
                col = (a * 2 + c2) * 16
                vcell[2 * ds + 2 + a, pl.ds(c2, 8, stride=2), :] = around[:, col : col + 16]

    clean = cells[0] - NOISE * vcell[...]
    cells[0] = clean
    first = firsts[:, 0:8, :].reshape(32, VAE)
    for dy, dx in taps():
        first += jnp.dot(
            window(cells, 0, dy, dx, 4), win_s[18 + dy * 3 + dx], preferred_element_type=F32
        )
    norm = lax.rsqrt(jnp.mean(first * first, axis=-1, keepdims=True) + 1e-6)
    z = first * norm * bias_ref[1:2, :]
    act = z / (1.0 + jnp.exp(-z))
    pos = iota((32, VAE), 0)
    y = 2 * s - 1 + pos // 8
    x = 6 * p - 1 + pos % 8
    inside = (y >= 0) & (y < 2 * NSEQ) & (x >= 0) & (x < 24)
    act = jnp.where(inside, act, 0.0)
    firsts[:, 0:8, :] = first.reshape(4, 8, VAE)
    acts[...] = jnp.zeros(acts.shape, F32)
    acts[0, :, 0:8, :] = act.reshape(4, 8, VAE)
    out = mid + firsts[1:3, 1:9, :].reshape(16, VAE)
    for dy, dx in taps():
        out += jnp.dot(
            window(acts, 0, dy, dx, 2), wmid_s[18 + dy * 3 + dx], preferred_element_type=F32
        )
    decoded_out[...] = out.reshape(2, 8, VAE)[:, 0:6, :]

    for c in range(CH):
        wait_bytes(qg.at[c, 0 : NSEQ - 1], q_send.at[c])
        wait_bytes(qg.at[c, 0 : NSEQ - 1], c_send.at[c])
        wait_bytes(qg.at[c, 0 : NSEQ - 1], d_send.at[c])

    @pl.when(same)
    def _():
        wait_bytes(er.at[0 : NSEQ - 1], e_send)

    @pl.when(jnp.logical_not(same))
    def _():
        wait_bytes(er, e_send)


def local(
    group_hidden,
    queries,
    history_keys,
    history_values,
    valid_len,
    out_weight,
    attn_gate,
    head_gain,
    head_shift,
    head_weight,
    head_bias,
    noisy_latent,
    prev_latent,
    prev_feat,
    conv_in_weight,
    conv_in_bias,
    vae_gain,
    conv_mid_weight,
    conv_mid_bias,
):
    start = lax.axis_index("sp") * FEAT
    gain = lax.dynamic_slice_in_dim(head_gain, start, FEAT, 0)
    shift = lax.dynamic_slice_in_dim(head_shift, start, FEAT, 0)
    zero = jnp.zeros_like(attn_gate)
    rows = jnp.stack([attn_gate, gain, shift] + [zero] * 5)
    none = jnp.zeros_like(vae_gain)
    biases = jnp.stack([conv_in_bias, vae_gain, conv_mid_bias] + [none] * 5)
    vecs = jnp.pad(head_bias[None], ((0, 7), (0, 64)))
    vmem = pl.BlockSpec(memory_space=pltpu.VMEM)
    hbm = pl.BlockSpec(memory_space=pl.ANY)
    smem = pl.BlockSpec(memory_space=pltpu.SMEM)
    blocks = (CH, NSEQ, PAD, CW)
    dma = pltpu.SemaphoreType.DMA
    return pl.pallas_call(
        kernel,
        out_shape=(
            jax.ShapeDtypeStruct((TOK, FEAT), BF16),
            jax.ShapeDtypeStruct((2, 6, VAE), F32),
        ),
        in_specs=[vmem, vmem, hbm, hbm, smem, hbm, vmem, vmem, vmem, hbm, vmem, vmem, vmem, hbm, hbm],
        out_specs=(vmem, vmem),
        scratch_shapes=[
            pltpu.VMEM((CH, HIST, CW), BF16),
            pltpu.VMEM((CH, HIST, CW), BF16),
            pltpu.VMEM((FEAT, COLS), BF16),
            pltpu.VMEM((FEAT, 64), F32),
            pltpu.VMEM((27, 16, VAE), BF16),
            pltpu.VMEM((27, VAE, VAE), BF16),
            pltpu.VMEM((CH, PAD, CW), BF16),
            pltpu.VMEM(blocks, BF16),
            pltpu.VMEM(blocks, BF16),
            pltpu.VMEM(blocks, BF16),
            pltpu.VMEM((CH, PAD, CW), BF16),
            pltpu.VMEM(blocks, BF16),
            pltpu.VMEM((NSEQ, PAD, 256), BF16),
            pltpu.VMEM((NSEQ, PAD, 256), BF16),
            pltpu.VMEM((PAD, HD), F32),
            pltpu.VMEM((3 * NSP, PAD, HD), F32),
            pltpu.VMEM((2, 8, HD), F32),
            pltpu.VMEM((9, 2, 8, HD), F32),
            pltpu.VMEM((32, VAE), BF16),
            pltpu.VMEM((9, 32, VAE), BF16),
            pltpu.VMEM((4, 8, VAE), F32),
            pltpu.VMEM((3, 6, 16, 16), F32),
            pltpu.VMEM((3, 24, HD), F32),
            pltpu.VMEM((6, 16, 16), F32),
            pltpu.VMEM((2, 4, 16, VAE), F32),
            pltpu.VMEM((4, 16, VAE), F32),
            pltpu.VMEM((1, 4, 16, VAE), F32),
            pltpu.VMEM((PAD, FEAT), F32),
            pltpu.VMEM((PAD, FEAT), F32),
            dma((CH,)),
            dma((CH,)),
            dma((4,)),
            dma((2 + 2 * CH,)),
            dma((CH,)),
            dma((CH,)),
            dma((CH,)),
            dma((CH,)),
            dma((CH,)),
            dma((CH,)),
            dma,
            dma,
            dma((3 * NSP,)),
            dma((3 * NSP,)),
            dma((9,)),
            dma((9,)),
            dma((9,)),
            dma((9,)),
        ],
        compiler_params=pltpu.CompilerParams(
            collective_id=0, has_side_effects=True, vmem_limit_bytes=56 << 20
        ),
    )(
        group_hidden,
        queries,
        history_keys,
        history_values,
        valid_len,
        out_weight,
        rows,
        vecs,
        biases,
        head_weight,
        noisy_latent,
        prev_latent,
        prev_feat,
        conv_in_weight.reshape(27, 16, VAE),
        conv_mid_weight.reshape(27, VAE, VAE),
    )


def solution(mesh):
    placed = (
        P("seq", "sp"),
        P("seq", "sp"),
        P("seq", "sp"),
        P("seq", "sp"),
        P("seq"),
        P("sp", "seq"),
        P("sp"),
        P(),
        P(),
        P(),
        P(),
        P("seq", "sp", None),
        P(None, "seq", "sp", None),
        P(None, "seq", "sp", None),
        P(),
        P(),
        P(),
        P(),
        P(),
    )
    return jax.shard_map(
        local,
        mesh=mesh,
        in_specs=placed,
        out_specs=(P("seq", "sp"), P("seq", "sp", None)),
        check_vma=False,
    )
```

```python
import functools
import math

import jax
import jax.numpy as jnp
from jax import lax
from jax.experimental import pallas as pl
from jax.experimental.pallas import tpu as pltpu
from jax.sharding import PartitionSpec as P

MESH = pl.DeviceIdType.MESH
BF16 = jnp.bfloat16
F32 = jnp.float32

D = 5120
HD = 128
NSEQ = 32
NSP = 4
TOK = 12
PAD = 16
TOKENS = NSEQ * TOK
HIST = 2048
FEAT = 1280
COLS = 160
CH = 5
CW = FEAT // CH
LINE = 4
PLANE = NSEQ // LINE
ROWS = PLANE * TOK
BY_Y = (False, True, False, True, False)
LAST = CH - 1
VAE = 384
EXP2_SCALE = math.log2(math.e) / math.sqrt(HD)
NOISE = 0.75


def iota(shape, dim):
    return lax.broadcasted_iota(jnp.int32, shape, dim)


def row_of(ref, start, count):
    return jnp.concatenate([ref[pl.ds(start + k, 1), :] for k in range(count)], axis=1)


def wait_bytes(region, sem):
    pltpu.make_async_copy(region, region, sem).wait()


def pad_rows(rows):
    width = rows.shape[-1]
    pairs = rows.reshape(-1, 2 * TOK, width)
    even = pairs[:, :PAD]
    odd = pltpu.roll(pairs, TOK, 1)[:, :PAD]
    return jnp.concatenate([even[:, None], odd[:, None]], axis=1).reshape(-1, PAD, width)


def pack_rows(blocks):
    width = blocks.shape[-1]
    pairs = blocks.reshape(-1, 2, PAD, width)
    zeros = jnp.zeros((pairs.shape[0], 8, width), F32)
    even = jnp.concatenate([pairs[:, 0], zeros], axis=1)
    odd = pltpu.roll(jnp.concatenate([pairs[:, 1], zeros], axis=1), TOK, 1)
    row = iota(even.shape, 1)
    return jnp.where(row < TOK, even, odd).reshape(-1, width)


def kernel(
    hidden_ref,
    q_ref,
    k_hbm,
    v_hbm,
    valid_ref,
    w_hbm,
    gate_ref,
    gain_ref,
    shift_ref,
    headb_ref,
    bias_in_ref,
    vgain_ref,
    bias_mid_ref,
    headw_hbm,
    noisy_ref,
    platent_ref,
    pfeat_ref,
    win_hbm,
    wmid_hbm,
    hidden_out,
    decoded_out,
    k_s,
    v_s,
    w_s,
    headw_s,
    headg_s,
    win_s,
    wmid_s,
    qs,
    qd,
    qp,
    ql,
    ao,
    agp,
    agl,
    pc,
    rc,
    ag,
    es,
    er,
    gs,
    gr,
    ls,
    lr,
    fs,
    fr,
    fpad,
    cells,
    vtok,
    vcell,
    feats,
    firsts,
    acts,
    proj,
    upd,
    ksem,
    vsem,
    wsem,
    lsem,
    q1_send,
    q1_recv,
    q2_send,
    q2_recv,
    d1_send,
    d1_recv,
    d2_send,
    d2_recv,
    c_send,
    c_recv,
    e_send,
    e_recv,
    g_send,
    g_recv,
    l_send,
    l_recv,
    f_send,
    f_recv,
):
    s = lax.axis_index("seq")
    p = lax.axis_index("sp")
    owner_sp = s // 8
    piece = lax.rem(s, 8)

    barrier = pltpu.get_barrier_semaphore()

    def greet(to_s, to_p):
        pl.semaphore_signal(barrier, inc=1, device_id=(to_s, to_p), device_id_type=MESH)

    def greet_seq(k, _):
        greet(lax.rem(s + k, NSEQ), p)
        return 0

    lax.fori_loop(1, NSEQ, greet_seq, 0)

    def greet_sources(k, _):
        greet(p * 8 + k // 3, lax.rem(p + 1 + lax.rem(k, 3), NSP))
        return 0

    lax.fori_loop(0, 24, greet_sources, 0)
    for ds in (-1, 0, 1):

        @pl.when(jnp.logical_and(s + ds >= 0, s + ds < NSEQ))
        def _():
            for dp in (1, 2, 3):
                greet(s + ds, lax.rem(p + dp, NSP))

    loads = []
    for c in range(CH):
        cols = pl.ds(c * CW, CW)
        kc = pltpu.make_async_copy(k_hbm.at[:, cols], k_s.at[c], ksem.at[c])
        vc = pltpu.make_async_copy(v_hbm.at[:, cols], v_s.at[c], vsem.at[c])
        kc.start()
        vc.start()
        loads.append((kc, vc))
    w_copy = pltpu.make_async_copy(w_hbm, w_s, wsem.at[0])
    head_cols = pl.ds(pl.multiple_of(p * FEAT, FEAT), FEAT)
    head_copy = pltpu.make_async_copy(headw_hbm.at[:, head_cols], headw_s, wsem.at[1])
    win_copy = pltpu.make_async_copy(win_hbm, win_s, wsem.at[2])
    wmid_copy = pltpu.make_async_copy(wmid_hbm, wmid_s, wsem.at[3])
    for copy in (win_copy, wmid_copy, w_copy, head_copy):
        copy.start()

    qs[...] = jnp.zeros(qs.shape, BF16)
    for c in range(CH):
        qs[c, 0:TOK, :] = q_ref[:, c * CW : (c + 1) * CW]
    x_at, y_at, z_at = s // 8, lax.rem(s // 2, 4), lax.rem(s, 2)

    def line_at(c):
        return y_at if BY_Y[c] else x_at

    def plane_at(c):
        return x_at * 2 + z_at if BY_Y[c] else y_at * 2 + z_at

    def line_peer(c, line):
        return x_at * 8 + line * 2 + z_at if BY_Y[c] else line * 8 + y_at * 2 + z_at

    def plane_peer(c, at):
        return (at // 2) * 8 + y_at * 2 + lax.rem(at, 2) if BY_Y[c] else x_at * 8 + at

    def to_line(c, buf, dst, send_sem, recv_sem, by_dest):
        for k in range(1, LINE):
            line = lax.rem(line_at(c) + k, LINE)
            pltpu.make_async_remote_copy(
                src_ref=buf.at[c, line if by_dest else line_at(c)],
                dst_ref=dst.at[c, line_at(c)],
                send_sem=send_sem.at[c],
                recv_sem=recv_sem.at[c],
                device_id=(line_peer(c, line), p),
                device_id_type=MESH,
            ).start()

    def to_plane(c, buf, dst, send_sem, recv_sem, by_dest):
        for k in range(1, PLANE):
            at = lax.rem(plane_at(c) + k, PLANE)
            pltpu.make_async_remote_copy(
                src_ref=buf.at[c, at] if by_dest else buf.at[c],
                dst_ref=dst.at[c, plane_at(c)],
                send_sem=send_sem.at[c],
                recv_sem=recv_sem.at[c],
                device_id=(plane_peer(c, at), p),
                device_id_type=MESH,
            ).start()

    def wait_line(c, dst, sem):
        wait_bytes(dst.at[c, 0 : LINE - 1], sem.at[c])

    def wait_plane(c, dst, sem):
        wait_bytes(dst.at[c, 0 : PLANE - 1], sem.at[c])

    ls[...] = jnp.zeros(ls.shape, F32)
    for x in range(6):
        ls[:, x, 0:16] = noisy_ref[x]
        ls[:, x, 16:32] = platent_ref[0, x].astype(F32)
        ls[:, x, 32:48] = platent_ref[1, x].astype(F32)
    fpad[...] = jnp.zeros(fpad.shape, F32)
    for f in range(2):
        for x in range(6):
            for r in range(2):
                fpad[2 * r + f, x, :] = pfeat_ref[f, x, r].astype(F32)
    fs[...] = fpad[...].reshape(2, 2 * 8, VAE).astype(BF16)

    rows_in = 1 + jnp.where(s > 0, 1, 0) + jnp.where(s < NSEQ - 1, 1, 0)
    pl.semaphore_wait(barrier, NSEQ - 1 + jnp.where(owner_sp != p, NSEQ, 0) + 3 * rows_in)

    def place(c, owner):
        if not BY_Y[c]:
            return owner
        return lax.rem(owner // 2, 4) * 8 + (owner // 8) * 2 + lax.rem(owner, 2)

    def to_all(src, dst, send_sem, recv_sem):
        def one(k, _):
            to = lax.rem(s + k, NSEQ)
            pltpu.make_async_remote_copy(
                src_ref=src(to),
                dst_ref=dst,
                send_sem=send_sem,
                recv_sem=recv_sem,
                device_id=(to, p),
                device_id_type=MESH,
            ).start()
            return 0

        lax.fori_loop(1, NSEQ, one, 0)

    def wait_all(dst, sem):
        wait_bytes(dst.at[0 : NSEQ - 1], sem)

    to_all(lambda to: qs.at[0], qd.at[s], q2_send.at[0], q2_recv.at[0])
    for c in range(1, CH):
        to_plane(c, qs, qp, q1_send, q1_recv, False)
    qd[pl.ds(s, 1)] = qs[0][None]

    def near(fn):
        for ds in (-1, 0, 1):
            for dp in (-1, 0, 1):
                if ds == 0 and dp == 0:
                    continue
                inside_s = jnp.logical_and(s + ds >= 0, s + ds < NSEQ)
                inside_p = jnp.logical_and(p + dp >= 0, p + dp < NSP)
                pl.when(jnp.logical_and(inside_s, inside_p))(functools.partial(fn, ds, dp))

    def slot_of(ds, dp):
        return (ds + 1) * 3 + dp + 1

    def border_copies(ds, dp):
        out, back = slot_of(ds, dp), slot_of(-ds, -dp)
        rows = {-1: slice(0, 1), 0: slice(0, 2), 1: slice(1, 2)}[ds]
        return [
            pltpu.make_async_remote_copy(
                src_ref=src,
                dst_ref=dst,
                send_sem=send.at[out],
                recv_sem=recv.at[back],
                device_id=(s + ds, p + dp),
                device_id_type=MESH,
            )
            for src, dst, send, recv in (
                (ls, lr.at[back], l_send, l_recv),
                (fs.at[rows], fr.at[back, rows], f_send, f_recv),
            )
        ]

    def border_start(ds, dp):
        for copy in border_copies(ds, dp):
            copy.start()

    def border_wait(ds, dp):
        slot = slot_of(ds, dp)
        part = fr.at[slot, 0:1] if ds else fr.at[slot]
        wait_bytes(lr.at[slot], l_recv.at[slot])
        wait_bytes(part, f_recv.at[slot])
        wait_bytes(lr.at[slot], l_send.at[slot])
        wait_bytes(part, f_send.at[slot])


    visible = iota((1, HIST), 1) < valid_ref[0]
    ones = jnp.ones((HIST, HD), BF16)
    half = TOKENS // 2
    lane = iota((half, HD), 1) % 32
    across = (((1,), (1,)), ((), ()))

    def spread_queries(c):
        qp[c, pl.ds(plane_at(c), 1)] = qs[c][None]
        wait_plane(c, qp, q1_recv)
        ql[c, pl.ds(line_at(c), 1)] = pack_rows(qp[c].astype(F32)).astype(BF16)[None]
        to_line(c, ql, ql, q2_send, q2_recv, False)

    def attend_ready(c):
        if c == 0:
            wait_all(qd, q2_recv.at[0])
        else:
            wait_line(c, ql, q2_recv)
        loads[c][0].wait()
        loads[c][1].wait()

    def spare_rows(st):
        at = iota(st.shape, 2)
        return jnp.where(
            at < 32,
            pltpu.roll(st, 12, 1),
            jnp.where(at < 64, pltpu.roll(st, 8, 1), pltpu.roll(st, 4, 1)),
        )

    def tokens_of(tile):
        at = iota(tile.shape, 1)
        return jnp.where(
            at < 4,
            pltpu.roll(tile, 4, 1),
            jnp.where(
                at < 8,
                pltpu.roll(pltpu.roll(tile, HD - 32, 2), 8, 1),
                pltpu.roll(pltpu.roll(tile, HD - 64, 2), 12, 1),
            ),
        )

    def attend(c):
        for r in range(2):
            owners = slice(r * (NSEQ // 2), (r + 1) * (NSEQ // 2))
            if c == 0:
                q = pack_rows(qd[owners].astype(F32)).astype(BF16)
            else:
                q = ql[c, 2 * r : 2 * r + 2].reshape(half, CW)
            stats = jnp.zeros((half, HD), F32)
            for h in range(2):
                cols = slice(h * HD, (h + 1) * HD)
                scores = lax.dot_general(
                    q[:, cols], k_s[c, :, cols], across, preferred_element_type=F32
                )
                scores = jnp.where(visible, scores, -1e30)
                top = jnp.max(scores, axis=1, keepdims=True) * EXP2_SCALE
                top = top.astype(BF16).astype(F32)
                weights = jnp.exp2(scores * EXP2_SCALE - top).astype(BF16)
                both = jnp.concatenate([v_s[c, :, cols], ones], axis=1)
                acc = jnp.dot(weights, both, preferred_element_type=F32)
                total = acc[:, HD:]
                high = total.astype(BF16).astype(F32)
                stats = jnp.where(lane == h, top, stats)
                stats = jnp.where(lane == 2 + h, high, stats)
                stats = jnp.where(lane == 4 + h, total - high, stats)
                tile = pad_rows(acc[:, :HD])
                if h == 1:
                    tile = jnp.where(iota(tile.shape, 1) < TOK, tile, spare_rows(pad_rows(stats)))
                pc[c, owners, :, cols] = tile.astype(BF16)

    def send_partials(c):
        rc[c, pl.ds(s, 1)] = pc[c, pl.ds(place(c, s), 1)]
        to_all(lambda to: pc.at[c, place(c, to)], rc.at[c, s], c_send.at[c], c_recv.at[c])

    def merge_owned(c, parts):
        st = tokens_of(parts[:, :, HD : 2 * HD].astype(F32))
        top = jnp.max(st, axis=0, keepdims=True)
        factor = jnp.exp2(st - top)
        sums = pltpu.roll(st, HD - 2, 2) + pltpu.roll(st, HD - 4, 2)
        factor = factor / jnp.sum(factor * sums, axis=0, keepdims=True)
        row = iota((PAD, HD), 0)
        for h in range(2):
            part = parts[:, :, h * HD : (h + 1) * HD].astype(F32)
            merged = jnp.sum(part * factor[:, :, h : h + 1], axis=0)
            merged = jnp.where(row < TOK, merged, 0.0)
            ao[c, :, h * HD : (h + 1) * HD] = merged.astype(BF16)

    def spread_attention(c):
        wait_plane(c, agp, d1_recv)
        agl[c, pl.ds(line_at(c), 1)] = pack_rows(agp[c].astype(F32)).astype(BF16)[None]
        to_line(c, agl, agl, d2_send, d2_recv, False)

    def merge(c):
        merge_owned(c, rc[c])
        if c == LAST:
            ag[pl.ds(s, 1)] = ao[c][None]
        else:
            agp[c, pl.ds(plane_at(c), 1)] = ao[c][None]

    def send_attention(c):
        if c == LAST:
            to_all(lambda to: ao.at[c], ag.at[s], d2_send.at[c], d2_recv.at[c])
        else:
            to_plane(c, ao, agp, d1_send, d1_recv, False)

    for c in range(1, CH):
        spread_queries(c)
    near(border_start)
    for c in range(CH):
        attend_ready(c)
        if c >= 3:
            wait_all(rc.at[c - 3], c_recv.at[c - 3])
        attend(c)
        if c >= 3:
            merge(c - 3)
        send_partials(c)
        if c >= 3:
            send_attention(c - 3)
    for c in range(2, CH):
        wait_all(rc.at[c], c_recv.at[c])
        merge(c)
        send_attention(c)
        spread_attention(c - 2)

    near(border_wait)
    win_copy.wait()
    wmid_copy.wait()
    lr[4] = ls[...]
    fr[4] = fs[...]
    cells[...] = jnp.zeros(cells.shape, F32)
    feats[...] = jnp.zeros(feats.shape, F32)
    for ds in (-1, 0, 1):
        for dp in (-1, 0, 1):
            inside = jnp.logical_and(
                jnp.logical_and(s + ds >= 0, s + ds < NSEQ),
                jnp.logical_and(p + dp >= 0, p + dp < NSP),
            )
            slot = slot_of(ds, dp)
            src = {-1: slice(4, 6), 0: slice(0, 6), 1: slice(0, 2)}[dp]
            dst = {-1: slice(0, 2), 0: slice(2, 8), 1: slice(8, 10)}[dp]
            for g in range(3):
                part = lr[slot, :, src, g * 16 : (g + 1) * 16]
                cells[g, 2 * ds + 2 : 2 * ds + 4, dst, :] = jnp.where(inside, part, 0.0)
            src = {-1: slice(5, 6), 0: slice(0, 6), 1: slice(0, 1)}[dp]
            dst = {-1: slice(0, 1), 0: slice(1, 7), 1: slice(7, 8)}[dp]
            part = fr[slot].astype(F32).reshape(2, 2, 8, VAE)
            part = jnp.where(inside, part, 0.0)
            rows = {-1: (1,), 0: (0, 1), 1: (0,)}[ds]
            for row in rows:
                for f in range(2):
                    feats[f, {-1: 0, 0: 1 + row, 1: 3}[ds], dst, :] = part[row, f, src, :]

    def window(ref, g, dy, dx, height):
        return ref[g, dy : dy + height, dx : dx + 8, :].reshape(height * 8, -1).astype(BF16)

    def taps():
        return [(dy, dx) for dy in range(3) for dx in range(3)]

    first = jnp.zeros((32, VAE), F32) + row_of(bias_in_ref, 0, 3)
    mid = jnp.zeros((16, VAE), F32) + row_of(bias_mid_ref, 0, 3)
    for f in range(2):
        for dy, dx in taps():
            tap = f * 9 + dy * 3 + dx
            first += jnp.dot(window(cells, f + 1, dy, dx, 4), win_s[tap], preferred_element_type=F32)
            mid += jnp.dot(window(feats, f, dy, dx, 2), wmid_s[tap], preferred_element_type=F32)
    firsts[:, 0:8, :] = first.reshape(4, 8, VAE)

    gate, gain = row_of(gate_ref, 0, 10), row_of(gain_ref, 10 * p, 10)
    shift = row_of(shift_ref, 10 * p, 10)
    head_copy.wait()
    headg_s[...] = headw_s[...] * gain
    fixed = lax.dot_general(
        jnp.where(iota((PAD, FEAT), 0) == TOK, gain, shift),
        headw_s[...],
        across,
        precision=lax.Precision.HIGHEST,
        preferred_element_type=F32,
    )
    upd[...] = jnp.zeros(upd.shape, F32)
    upd[0:TOK, :] = hidden_ref[...].astype(F32)

    w_copy.wait()

    def agl_ready(c):
        wait_line(c, agl, d2_recv)
        return agl[c].reshape(TOKENS, CW)

    def project(c, block):
        cols = w_s[:, c * CW : (c + 1) * CW]
        return lax.dot_general(block, cols, across, preferred_element_type=F32)

    by_x = pad_rows(project(0, agl_ready(0)) + project(2, agl_ready(2)))
    by_y = project(1, agl_ready(1))
    spread_attention(3)
    by_y = pad_rows(by_y + project(3, agl_ready(3))).reshape(4, 4, 2, PAD, COLS)
    result = by_x + jnp.stack([by_y[:, x] for x in range(4)]).reshape(NSEQ, PAD, COLS)
    wait_all(ag, d2_recv.at[LAST])
    result += project(LAST, ag[...].reshape(NSEQ * PAD, CW)).reshape(NSEQ, PAD, COLS)
    rest = jnp.concatenate([result[:, :, HD:], jnp.zeros((NSEQ, PAD, 2 * HD - COLS), F32)], axis=2)
    rest = rest + pltpu.roll(rest, 32, 2) + pltpu.roll(rest, 64, 2)
    tile = jnp.where(iota(rest.shape, 1) < TOK, result[:, :, :HD], spare_rows(rest))
    es[...] = tile.astype(BF16)
    e_slot = piece * NSP + p
    same = owner_sp == p

    def send_piece(k, _):
        to = lax.rem(s + k, NSEQ)
        pltpu.make_async_remote_copy(
            src_ref=es.at[to],
            dst_ref=er.at[e_slot],
            send_sem=e_send,
            recv_sem=e_recv,
            device_id=(to, owner_sp),
            device_id_type=MESH,
        ).start()
        return 0

    lax.fori_loop(1, NSEQ, send_piece, 0)

    @pl.when(same)
    def _():
        own = pltpu.make_async_copy(es.at[s], er.at[e_slot], lsem.at[0])
        own.start()
        own.wait()
        wait_bytes(er.at[0 : NSEQ - 1], e_recv)

    @pl.when(jnp.logical_not(same))
    def _():
        send_piece(0, 0)
        wait_bytes(er, e_recv)

    pieces = jnp.sum(er[...].astype(F32).reshape(8, NSP, PAD, HD), axis=1)
    rests = tokens_of(pieces)
    for j in range(8):
        proj[:, j * COLS : j * COLS + HD] = pieces[j]
        proj[:, j * COLS + HD : (j + 1) * COLS] = rests[j, :, 0 : COLS - HD]
    updated = jnp.where(iota((PAD, FEAT), 0) < TOK, upd[...] + gate * proj[...], 0.0)
    hidden_out[...] = updated[0:TOK].astype(BF16)
    part = lax.dot_general(
        updated,
        headg_s[...],
        across,
        precision=lax.Precision.HIGHEST,
        preferred_element_type=F32,
    )
    part = jnp.where(iota((PAD, 64), 0) < TOK, part, fixed)
    gs[...] = jnp.zeros(gs.shape, F32)
    gs[:, 0:64] = part
    gs[:, 64:65] = jnp.sum(updated, axis=1, keepdims=True)
    gs[:, 65:66] = jnp.sum(updated * updated, axis=1, keepdims=True)

    def share(fn):
        for ds in (-1, 0, 1):
            for dp in range(NSP):
                if ds == 0 and dp == 0:
                    continue
                inside = jnp.logical_and(s + ds >= 0, s + ds < NSEQ)
                pl.when(inside)(functools.partial(fn, ds, dp))

    def g_start(ds, dp):
        pltpu.make_async_remote_copy(
            src_ref=gs,
            dst_ref=gr.at[(1 - ds) * NSP + dp],
            send_sem=g_send.at[(ds + 1) * NSP + dp],
            recv_sem=g_recv.at[(1 - ds) * NSP + dp],
            device_id=(s + ds, lax.rem(p + dp, NSP)),
            device_id_type=MESH,
        ).start()

    def g_wait(ds, dp):
        slot = (ds + 1) * NSP + dp
        wait_bytes(gr.at[slot], g_recv.at[slot])
        wait_bytes(gr.at[slot], g_send.at[slot])

    share(g_start)
    gr[NSP] = gs[...]
    share(g_wait)

    vtok[...] = jnp.zeros(vtok.shape, F32)
    vcell[...] = jnp.zeros(vcell.shape, F32)
    for ds in (-1, 0, 1):
        inside = jnp.logical_and(s + ds >= 0, s + ds < NSEQ)
        total = gr[(ds + 1) * NSP]
        for dp in range(1, NSP):
            total = total + gr[(ds + 1) * NSP + dp]
        mean = total[0:TOK, 64:65] / D
        var = total[0:TOK, 65:66] / D - mean * mean
        scaled = (total[0:TOK, 0:64] - mean * total[12:13, 0:64]) * lax.rsqrt(var + 1e-6)
        velocity = scaled + total[13:14, 0:64] + headb_ref[...]
        vtok[ds + 1, 1 : TOK + 1, 0:64] = jnp.where(inside, velocity, 0.0)
        around = vtok[ds + 1, pl.ds(3 * p, 8), :]
        for a in range(2):
            for c2 in range(2):
                col = (a * 2 + c2) * 16
                vcell[2 * ds + 2 + a, pl.ds(c2, 8, stride=2), :] = around[:, col : col + 16]

    clean = cells[0] - NOISE * vcell[...]
    cells[0] = clean
    first = firsts[:, 0:8, :].reshape(32, VAE)
    for dy, dx in taps():
        first += jnp.dot(
            window(cells, 0, dy, dx, 4), win_s[18 + dy * 3 + dx], preferred_element_type=F32
        )
    norm = lax.rsqrt(jnp.mean(first * first, axis=-1, keepdims=True) + 1e-6)
    z = first * norm * row_of(vgain_ref, 0, 3)
    act = z / (1.0 + jnp.exp(-z))
    pos = iota((32, VAE), 0)
    y = 2 * s - 1 + pos // 8
    x = 6 * p - 1 + pos % 8
    inside = (y >= 0) & (y < 2 * NSEQ) & (x >= 0) & (x < 24)
    act = jnp.where(inside, act, 0.0)
    firsts[:, 0:8, :] = first.reshape(4, 8, VAE)
    acts[...] = jnp.zeros(acts.shape, F32)
    acts[0, :, 0:8, :] = act.reshape(4, 8, VAE)
    out = mid + firsts[1:3, 1:9, :].reshape(16, VAE)
    for dy, dx in taps():
        out += jnp.dot(
            window(acts, 0, dy, dx, 2), wmid_s[18 + dy * 3 + dx], preferred_element_type=F32
        )
    out = out.reshape(2, 8, VAE)
    for x in range(6):
        decoded_out[x] = out[:, x, :]

    wait_all(qd, q2_send.at[0])
    for c in range(CH):
        wait_all(rc.at[c], c_send.at[c])
        if c > 0:
            wait_plane(c, qp, q1_send)
            wait_line(c, ql, q2_send)
        if c < LAST:
            wait_plane(c, agp, d1_send)
            wait_line(c, agl, d2_send)
    wait_all(ag, d2_send.at[LAST])

    @pl.when(same)
    def _():
        wait_bytes(er.at[0 : NSEQ - 1], e_send)

    @pl.when(jnp.logical_not(same))
    def _():
        wait_bytes(er, e_send)


def local(
    group_hidden,
    queries,
    history_keys,
    history_values,
    valid_len,
    out_weight,
    attn_gate,
    head_gain,
    head_shift,
    head_weight,
    head_bias,
    noisy_latent,
    prev_latent,
    prev_feat,
    conv_in_weight,
    conv_in_bias,
    vae_gain,
    conv_mid_weight,
    conv_mid_bias,
):
    vmem = pl.BlockSpec(memory_space=pltpu.VMEM)
    hbm = pl.BlockSpec(memory_space=pl.ANY)
    smem = pl.BlockSpec(memory_space=pltpu.SMEM)
    dma = pltpu.SemaphoreType.DMA
    hidden, decoded = pl.pallas_call(
        kernel,
        out_shape=(
            jax.ShapeDtypeStruct((TOK, FEAT), BF16),
            jax.ShapeDtypeStruct((6, 2, VAE), F32),
        ),
        in_specs=[vmem, vmem, hbm, hbm, smem, hbm] + [vmem] * 7 + [hbm, vmem, vmem, vmem, hbm, hbm],
        out_specs=(vmem, vmem),
        scratch_shapes=[
            pltpu.VMEM((CH, HIST, CW), BF16),
            pltpu.VMEM((CH, HIST, CW), BF16),
            pltpu.VMEM((COLS, FEAT), BF16),
            pltpu.VMEM((64, FEAT), F32),
            pltpu.VMEM((64, FEAT), F32),
            pltpu.VMEM((27, 16, VAE), BF16),
            pltpu.VMEM((27, VAE, VAE), BF16),
            pltpu.VMEM((CH, PAD, CW), BF16),
            pltpu.VMEM((NSEQ, PAD, CW), BF16),
            pltpu.VMEM((CH, PLANE, PAD, CW), BF16),
            pltpu.VMEM((CH, LINE, ROWS, CW), BF16),
            pltpu.VMEM((CH, PAD, CW), BF16),
            pltpu.VMEM((CH, PLANE, PAD, CW), BF16),
            pltpu.VMEM((CH, LINE, ROWS, CW), BF16),
            pltpu.VMEM((CH, NSEQ, PAD, CW), BF16),
            pltpu.VMEM((CH, NSEQ, PAD, CW), BF16),
            pltpu.VMEM((NSEQ, PAD, CW), BF16),
            pltpu.VMEM((NSEQ, PAD, HD), BF16),
            pltpu.VMEM((NSEQ, PAD, HD), BF16),
            pltpu.VMEM((PAD, HD), F32),
            pltpu.VMEM((3 * NSP, PAD, HD), F32),
            pltpu.VMEM((2, 8, HD), F32),
            pltpu.VMEM((9, 2, 8, HD), F32),
            pltpu.VMEM((2, 16, VAE), BF16),
            pltpu.VMEM((9, 2, 16, VAE), BF16),
            pltpu.VMEM((4, 8, VAE), F32),
            pltpu.VMEM((3, 6, 16, 16), F32),
            pltpu.VMEM((3, 24, HD), F32),
            pltpu.VMEM((6, 16, 16), F32),
            pltpu.VMEM((2, 4, 16, VAE), F32),
            pltpu.VMEM((4, 16, VAE), F32),
            pltpu.VMEM((1, 4, 16, VAE), F32),
            pltpu.VMEM((PAD, FEAT), F32),
            pltpu.VMEM((PAD, FEAT), F32),
            dma((CH,)),
            dma((CH,)),
            dma((4,)),
            dma((1,)),
        ]
        + [dma((CH,))] * 10
        + [
            dma,
            dma,
            dma((3 * NSP,)),
            dma((3 * NSP,)),
            dma((9,)),
            dma((9,)),
            dma((9,)),
            dma((9,)),
        ],
        compiler_params=pltpu.CompilerParams(
            collective_id=0, has_side_effects=True, vmem_limit_bytes=56 << 20
        ),
    )(
        group_hidden,
        queries,
        history_keys,
        history_values,
        valid_len,
        out_weight.T,
        attn_gate.reshape(-1, HD),
        head_gain.reshape(-1, HD),
        head_shift.reshape(-1, HD),
        head_bias.reshape(1, -1),
        conv_in_bias.reshape(-1, HD),
        vae_gain.reshape(-1, HD),
        conv_mid_bias.reshape(-1, HD),
        head_weight.T,
        noisy_latent.transpose(1, 0, 2),
        prev_latent.transpose(0, 2, 1, 3),
        prev_feat.transpose(0, 2, 1, 3),
        conv_in_weight.reshape(27, 16, VAE),
        conv_mid_weight.reshape(27, VAE, VAE),
    )
    return hidden, decoded.transpose(1, 0, 2)


def solution(mesh):
    placed = (
        P("seq", "sp"),
        P("seq", "sp"),
        P("seq", "sp"),
        P("seq", "sp"),
        P("seq"),
        P("sp", "seq"),
        P("sp"),
        P(),
        P(),
        P(),
        P(),
        P("seq", "sp", None),
        P(None, "seq", "sp", None),
        P(None, "seq", "sp", None),
        P(),
        P(),
        P(),
        P(),
        P(),
    )
    return jax.shard_map(
        local,
        mesh=mesh,
        in_specs=placed,
        out_specs=(P("seq", "sp"), P("seq", "sp", None)),
        check_vma=False,
    )
```

```python
import functools
import math

import jax
import jax.numpy as jnp
from jax import lax
from jax.experimental import pallas as pl
from jax.experimental.pallas import tpu as pltpu
from jax.sharding import PartitionSpec as P

MESH = pl.DeviceIdType.MESH
BF16 = jnp.bfloat16
F32 = jnp.float32

D = 5120
HD = 128
NSEQ = 32
NSP = 4
TOK = 12
PAD = 16
TOKENS = NSEQ * TOK
HIST = 2048
FEAT = 1280
COLS = 160
CH = 5
CW = FEAT // CH
LINE = 4
PLANE = NSEQ // LINE
ROWS = PLANE * TOK
BY_Y = (False, True, False, True, False)
LAST = CH - 1
VAE = 384
EXP2_SCALE = math.log2(math.e) / math.sqrt(HD)
NOISE = 0.75


def iota(shape, dim):
    return lax.broadcasted_iota(jnp.int32, shape, dim)


def row_of(ref, start, count):
    return jnp.concatenate([ref[pl.ds(start + k, 1), :] for k in range(count)], axis=1)


def wait_bytes(region, sem):
    pltpu.make_async_copy(region, region, sem).wait()


def pad_rows(rows):
    width = rows.shape[-1]
    pairs = rows.reshape(-1, 2 * TOK, width)
    even = pairs[:, :PAD]
    odd = pltpu.roll(pairs, TOK, 1)[:, :PAD]
    return jnp.concatenate([even[:, None], odd[:, None]], axis=1).reshape(-1, PAD, width)


def pack_rows(blocks):
    width = blocks.shape[-1]
    pairs = blocks.reshape(-1, 2, PAD, width)
    zeros = jnp.zeros((pairs.shape[0], 8, width), F32)
    even = jnp.concatenate([pairs[:, 0], zeros], axis=1)
    odd = pltpu.roll(jnp.concatenate([pairs[:, 1], zeros], axis=1), TOK, 1)
    row = iota(even.shape, 1)
    return jnp.where(row < TOK, even, odd).reshape(-1, width)


def kernel(
    hidden_ref,
    q_ref,
    k_hbm,
    v_hbm,
    valid_ref,
    w_hbm,
    gate_ref,
    gain_ref,
    shift_ref,
    headb_ref,
    bias_in_ref,
    vgain_ref,
    bias_mid_ref,
    headw_hbm,
    noisy_ref,
    platent_ref,
    pfeat_ref,
    win_hbm,
    wmid_hbm,
    hidden_out,
    decoded_out,
    k_s,
    v_s,
    w_s,
    headw_s,
    headg_s,
    win_s,
    wmid_s,
    qs,
    qd,
    qp,
    ql,
    ao,
    agp,
    agl,
    pc,
    rc,
    ag,
    es,
    er,
    gs,
    gr,
    ls,
    lr,
    fs,
    fr,
    fpad,
    cells,
    vtok,
    vcell,
    feats,
    firsts,
    acts,
    proj,
    upd,
    ksem,
    vsem,
    wsem,
    lsem,
    q1_send,
    q1_recv,
    q2_send,
    q2_recv,
    d1_send,
    d1_recv,
    d2_send,
    d2_recv,
    c_send,
    c_recv,
    e_send,
    e_recv,
    g_send,
    g_recv,
    l_send,
    l_recv,
    f_send,
    f_recv,
):
    s = lax.axis_index("seq")
    p = lax.axis_index("sp")
    owner_sp = s // 8
    piece = lax.rem(s, 8)

    barrier = pltpu.get_barrier_semaphore()

    def greet(to_s, to_p):
        pl.semaphore_signal(barrier, inc=1, device_id=(to_s, to_p), device_id_type=MESH)

    def greet_seq(k, _):
        greet(lax.rem(s + k, NSEQ), p)
        return 0

    lax.fori_loop(1, NSEQ, greet_seq, 0)

    def greet_sources(k, _):
        greet(p * 8 + k // 3, lax.rem(p + 1 + lax.rem(k, 3), NSP))
        return 0

    lax.fori_loop(0, 24, greet_sources, 0)
    for ds in (-1, 0, 1):

        @pl.when(jnp.logical_and(s + ds >= 0, s + ds < NSEQ))
        def _():
            for dp in (1, 2, 3):
                greet(s + ds, lax.rem(p + dp, NSP))

    loads = []
    for c in range(CH):
        cols = pl.ds(c * CW, CW)
        kc = pltpu.make_async_copy(k_hbm.at[:, cols], k_s.at[c], ksem.at[c])
        vc = pltpu.make_async_copy(v_hbm.at[:, cols], v_s.at[c], vsem.at[c])
        kc.start()
        vc.start()
        loads.append((kc, vc))
    w_copy = pltpu.make_async_copy(w_hbm, w_s, wsem.at[0])
    head_cols = pl.ds(pl.multiple_of(p * FEAT, FEAT), FEAT)
    head_copy = pltpu.make_async_copy(headw_hbm.at[:, head_cols], headw_s, wsem.at[1])
    win_copy = pltpu.make_async_copy(win_hbm, win_s, wsem.at[2])
    wmid_copy = pltpu.make_async_copy(wmid_hbm, wmid_s, wsem.at[3])
    for copy in (win_copy, wmid_copy, w_copy, head_copy):
        copy.start()

    qs[...] = jnp.zeros(qs.shape, BF16)
    for c in range(CH):
        qs[c, 0:TOK, :] = q_ref[:, c * CW : (c + 1) * CW]
    x_at, y_at, z_at = s // 8, lax.rem(s // 2, 4), lax.rem(s, 2)

    def line_at(c):
        return y_at if BY_Y[c] else x_at

    def plane_at(c):
        return x_at * 2 + z_at if BY_Y[c] else y_at * 2 + z_at

    def line_peer(c, line):
        return x_at * 8 + line * 2 + z_at if BY_Y[c] else line * 8 + y_at * 2 + z_at

    def plane_peer(c, at):
        return (at // 2) * 8 + y_at * 2 + lax.rem(at, 2) if BY_Y[c] else x_at * 8 + at

    def to_line(c, buf, dst, send_sem, recv_sem, by_dest):
        for k in range(1, LINE):
            line = lax.rem(line_at(c) + k, LINE)
            pltpu.make_async_remote_copy(
                src_ref=buf.at[c, line if by_dest else line_at(c)],
                dst_ref=dst.at[c, line_at(c)],
                send_sem=send_sem.at[c],
                recv_sem=recv_sem.at[c],
                device_id=(line_peer(c, line), p),
                device_id_type=MESH,
            ).start()

    def to_plane(c, buf, dst, send_sem, recv_sem, by_dest):
        for k in range(1, PLANE):
            at = lax.rem(plane_at(c) + k, PLANE)
            pltpu.make_async_remote_copy(
                src_ref=buf.at[c, at] if by_dest else buf.at[c],
                dst_ref=dst.at[c, plane_at(c)],
                send_sem=send_sem.at[c],
                recv_sem=recv_sem.at[c],
                device_id=(plane_peer(c, at), p),
                device_id_type=MESH,
            ).start()

    def wait_line(c, dst, sem):
        wait_bytes(dst.at[c, 0 : LINE - 1], sem.at[c])

    def wait_plane(c, dst, sem):
        wait_bytes(dst.at[c, 0 : PLANE - 1], sem.at[c])

    ls[...] = jnp.zeros(ls.shape, F32)
    for x in range(6):
        ls[:, x, 0:16] = noisy_ref[x]
        ls[:, x, 16:32] = platent_ref[0, x].astype(F32)
        ls[:, x, 32:48] = platent_ref[1, x].astype(F32)
    fpad[...] = jnp.zeros(fpad.shape, F32)
    for f in range(2):
        for x in range(6):
            for r in range(2):
                fpad[2 * r + f, x, :] = pfeat_ref[f, x, r].astype(F32)
    fs[...] = fpad[...].reshape(2, 2 * 8, VAE).astype(BF16)

    rows_in = 1 + jnp.where(s > 0, 1, 0) + jnp.where(s < NSEQ - 1, 1, 0)
    pl.semaphore_wait(barrier, NSEQ - 1 + jnp.where(owner_sp != p, NSEQ, 0) + 3 * rows_in)

    def place(c, owner):
        if not BY_Y[c]:
            return owner
        return lax.rem(owner // 2, 4) * 8 + (owner // 8) * 2 + lax.rem(owner, 2)

    def to_all(src, dst, send_sem, recv_sem):
        def one(k, _):
            to = lax.rem(s + k, NSEQ)
            pltpu.make_async_remote_copy(
                src_ref=src(to),
                dst_ref=dst,
                send_sem=send_sem,
                recv_sem=recv_sem,
                device_id=(to, p),
                device_id_type=MESH,
            ).start()
            return 0

        lax.fori_loop(1, NSEQ, one, 0)

    def wait_all(dst, sem):
        wait_bytes(dst.at[0 : NSEQ - 1], sem)

    to_all(lambda to: qs.at[0], qd.at[s], q2_send.at[0], q2_recv.at[0])
    for c in range(1, CH):
        to_plane(c, qs, qp, q1_send, q1_recv, False)
    qd[pl.ds(s, 1)] = qs[0][None]

    def near(fn):
        for ds in (-1, 0, 1):
            for dp in (-1, 0, 1):
                if ds == 0 and dp == 0:
                    continue
                inside_s = jnp.logical_and(s + ds >= 0, s + ds < NSEQ)
                inside_p = jnp.logical_and(p + dp >= 0, p + dp < NSP)
                pl.when(jnp.logical_and(inside_s, inside_p))(functools.partial(fn, ds, dp))

    def slot_of(ds, dp):
        return (ds + 1) * 3 + dp + 1

    def border_copies(ds, dp):
        out, back = slot_of(ds, dp), slot_of(-ds, -dp)
        rows = {-1: slice(0, 1), 0: slice(0, 2), 1: slice(1, 2)}[ds]
        return [
            pltpu.make_async_remote_copy(
                src_ref=src,
                dst_ref=dst,
                send_sem=send.at[out],
                recv_sem=recv.at[back],
                device_id=(s + ds, p + dp),
                device_id_type=MESH,
            )
            for src, dst, send, recv in (
                (ls, lr.at[back], l_send, l_recv),
                (fs.at[rows], fr.at[back, rows], f_send, f_recv),
            )
        ]

    def border_start(ds, dp):
        for copy in border_copies(ds, dp):
            copy.start()

    def border_wait(ds, dp):
        slot = slot_of(ds, dp)
        part = fr.at[slot, 0:1] if ds else fr.at[slot]
        wait_bytes(lr.at[slot], l_recv.at[slot])
        wait_bytes(part, f_recv.at[slot])
        wait_bytes(lr.at[slot], l_send.at[slot])
        wait_bytes(part, f_send.at[slot])


    visible = iota((1, HIST), 1) < valid_ref[0]
    ones = jnp.ones((HIST, HD), BF16)
    half = TOKENS // 2
    lane = iota((half, HD), 1) % 32
    across = (((1,), (1,)), ((), ()))

    def spread_queries(c):
        qp[c, pl.ds(plane_at(c), 1)] = qs[c][None]
        wait_plane(c, qp, q1_recv)
        ql[c, pl.ds(line_at(c), 1)] = pack_rows(qp[c].astype(F32)).astype(BF16)[None]
        to_line(c, ql, ql, q2_send, q2_recv, False)

    def attend_ready(c):
        if c == 0:
            wait_all(qd, q2_recv.at[0])
        else:
            wait_line(c, ql, q2_recv)
        loads[c][0].wait()
        loads[c][1].wait()

    def spare_rows(st):
        at = iota(st.shape, 2)
        return jnp.where(
            at < 32,
            pltpu.roll(st, 12, 1),
            jnp.where(at < 64, pltpu.roll(st, 8, 1), pltpu.roll(st, 4, 1)),
        )

    def tokens_of(tile):
        at = iota(tile.shape, 1)
        return jnp.where(
            at < 4,
            pltpu.roll(tile, 4, 1),
            jnp.where(
                at < 8,
                pltpu.roll(pltpu.roll(tile, HD - 32, 2), 8, 1),
                pltpu.roll(pltpu.roll(tile, HD - 64, 2), 12, 1),
            ),
        )

    def attend(c):
        for r in range(2):
            owners = slice(r * (NSEQ // 2), (r + 1) * (NSEQ // 2))
            if c == 0:
                q = pack_rows(qd[owners].astype(F32)).astype(BF16)
            else:
                q = ql[c, 2 * r : 2 * r + 2].reshape(half, CW)
            stats = jnp.zeros((half, HD), F32)
            for h in range(2):
                cols = slice(h * HD, (h + 1) * HD)
                scores = lax.dot_general(
                    q[:, cols], k_s[c, :, cols], across, preferred_element_type=F32
                )
                scores = jnp.where(visible, scores, -1e30)
                top = jnp.max(scores, axis=1, keepdims=True) * EXP2_SCALE
                top = top.astype(BF16).astype(F32)
                weights = jnp.exp2(scores * EXP2_SCALE - top).astype(BF16)
                both = jnp.concatenate([v_s[c, :, cols], ones], axis=1)
                acc = jnp.dot(weights, both, preferred_element_type=F32)
                total = acc[:, HD:]
                high = total.astype(BF16).astype(F32)
                stats = jnp.where(lane == h, top, stats)
                stats = jnp.where(lane == 2 + h, high, stats)
                stats = jnp.where(lane == 4 + h, total - high, stats)
                tile = pad_rows(acc[:, :HD])
                if h == 1:
                    tile = jnp.where(iota(tile.shape, 1) < TOK, tile, spare_rows(pad_rows(stats)))
                pc[c, owners, :, cols] = tile.astype(BF16)

    def send_partials(c):
        rc[c, pl.ds(s, 1)] = pc[c, pl.ds(place(c, s), 1)]
        to_all(lambda to: pc.at[c, place(c, to)], rc.at[c, s], c_send.at[c], c_recv.at[c])

    def merge_owned(c, parts):
        st = tokens_of(parts[:, :, HD : 2 * HD].astype(F32))
        top = jnp.max(st, axis=0, keepdims=True)
        factor = jnp.exp2(st - top)
        sums = pltpu.roll(st, HD - 2, 2) + pltpu.roll(st, HD - 4, 2)
        factor = factor / jnp.sum(factor * sums, axis=0, keepdims=True)
        row = iota((PAD, HD), 0)
        for h in range(2):
            part = parts[:, :, h * HD : (h + 1) * HD].astype(F32)
            merged = jnp.sum(part * factor[:, :, h : h + 1], axis=0)
            merged = jnp.where(row < TOK, merged, 0.0)
            ao[c, :, h * HD : (h + 1) * HD] = merged.astype(BF16)

    def spread_attention(c):
        wait_plane(c, agp, d1_recv)
        agl[c, pl.ds(line_at(c), 1)] = pack_rows(agp[c].astype(F32)).astype(BF16)[None]
        to_line(c, agl, agl, d2_send, d2_recv, False)

    def merge(c):
        merge_owned(c, rc[c])
        if c == LAST:
            ag[pl.ds(s, 1)] = ao[c][None]
        else:
            agp[c, pl.ds(plane_at(c), 1)] = ao[c][None]

    def send_attention(c):
        if c == LAST:
            to_all(lambda to: ao.at[c], ag.at[s], d2_send.at[c], d2_recv.at[c])
        else:
            to_plane(c, ao, agp, d1_send, d1_recv, False)

    for c in range(1, CH):
        spread_queries(c)
    near(border_start)
    for c in range(CH):
        attend_ready(c)
        if c >= 3:
            wait_all(rc.at[c - 3], c_recv.at[c - 3])
        attend(c)
        if c >= 3:
            merge(c - 3)
        send_partials(c)
        if c >= 3:
            send_attention(c - 3)
    spread_attention(0)

    near(border_wait)
    win_copy.wait()
    wmid_copy.wait()
    lr[4] = ls[...]
    fr[4] = fs[...]
    cells[...] = jnp.zeros(cells.shape, F32)
    feats[...] = jnp.zeros(feats.shape, F32)
    for ds in (-1, 0, 1):
        for dp in (-1, 0, 1):
            inside = jnp.logical_and(
                jnp.logical_and(s + ds >= 0, s + ds < NSEQ),
                jnp.logical_and(p + dp >= 0, p + dp < NSP),
            )
            slot = slot_of(ds, dp)
            src = {-1: slice(4, 6), 0: slice(0, 6), 1: slice(0, 2)}[dp]
            dst = {-1: slice(0, 2), 0: slice(2, 8), 1: slice(8, 10)}[dp]
            for g in range(3):
                part = lr[slot, :, src, g * 16 : (g + 1) * 16]
                cells[g, 2 * ds + 2 : 2 * ds + 4, dst, :] = jnp.where(inside, part, 0.0)
            src = {-1: slice(5, 6), 0: slice(0, 6), 1: slice(0, 1)}[dp]
            dst = {-1: slice(0, 1), 0: slice(1, 7), 1: slice(7, 8)}[dp]
            part = fr[slot].astype(F32).reshape(2, 2, 8, VAE)
            part = jnp.where(inside, part, 0.0)
            rows = {-1: (1,), 0: (0, 1), 1: (0,)}[ds]
            for row in rows:
                for f in range(2):
                    feats[f, {-1: 0, 0: 1 + row, 1: 3}[ds], dst, :] = part[row, f, src, :]

    def window(ref, g, dy, dx, height):
        return ref[g, dy : dy + height, dx : dx + 8, :].reshape(height * 8, -1).astype(BF16)

    def taps():
        return [(dy, dx) for dy in range(3) for dx in range(3)]

    first = jnp.zeros((32, VAE), F32) + row_of(bias_in_ref, 0, 3)
    mid = jnp.zeros((16, VAE), F32) + row_of(bias_mid_ref, 0, 3)
    for f in range(2):
        for dy, dx in taps():
            tap = f * 9 + dy * 3 + dx
            first += jnp.dot(window(cells, f + 1, dy, dx, 4), win_s[tap], preferred_element_type=F32)
            mid += jnp.dot(window(feats, f, dy, dx, 2), wmid_s[tap], preferred_element_type=F32)
    firsts[:, 0:8, :] = first.reshape(4, 8, VAE)

    def merge_and_send(c):
        wait_all(rc.at[c], c_recv.at[c])
        merge(c)
        send_attention(c)

    merge_and_send(2)
    spread_attention(1)
    merge_and_send(3)
    spread_attention(2)

    gate, gain = row_of(gate_ref, 0, 10), row_of(gain_ref, 10 * p, 10)
    shift = row_of(shift_ref, 10 * p, 10)
    head_copy.wait()
    headg_s[...] = headw_s[...] * gain
    fixed = lax.dot_general(
        jnp.where(iota((PAD, FEAT), 0) == TOK, gain, shift),
        headw_s[...],
        across,
        precision=lax.Precision.HIGHEST,
        preferred_element_type=F32,
    )
    upd[...] = jnp.zeros(upd.shape, F32)
    upd[0:TOK, :] = hidden_ref[...].astype(F32)

    spread_attention(3)
    merge_and_send(LAST)

    w_copy.wait()

    def agl_ready(c):
        wait_line(c, agl, d2_recv)
        return agl[c].reshape(TOKENS, CW)

    def project(c, block):
        cols = w_s[:, c * CW : (c + 1) * CW]
        return lax.dot_general(block, cols, across, preferred_element_type=F32)

    by_x = pad_rows(project(0, agl_ready(0)) + project(2, agl_ready(2)))
    by_y = project(1, agl_ready(1))
    by_y = pad_rows(by_y + project(3, agl_ready(3))).reshape(4, 4, 2, PAD, COLS)
    result = by_x + jnp.stack([by_y[:, x] for x in range(4)]).reshape(NSEQ, PAD, COLS)
    wait_all(ag, d2_recv.at[LAST])
    result += project(LAST, ag[...].reshape(NSEQ * PAD, CW)).reshape(NSEQ, PAD, COLS)
    rest = jnp.concatenate([result[:, :, HD:], jnp.zeros((NSEQ, PAD, 2 * HD - COLS), F32)], axis=2)
    rest = rest + pltpu.roll(rest, 32, 2) + pltpu.roll(rest, 64, 2)
    tile = jnp.where(iota(rest.shape, 1) < TOK, result[:, :, :HD], spare_rows(rest))
    es[...] = tile.astype(BF16)
    e_slot = piece * NSP + p
    same = owner_sp == p

    def send_piece(k, _):
        to = lax.rem(s + k, NSEQ)
        pltpu.make_async_remote_copy(
            src_ref=es.at[to],
            dst_ref=er.at[e_slot],
            send_sem=e_send,
            recv_sem=e_recv,
            device_id=(to, owner_sp),
            device_id_type=MESH,
        ).start()
        return 0

    lax.fori_loop(1, NSEQ, send_piece, 0)

    @pl.when(same)
    def _():
        own = pltpu.make_async_copy(es.at[s], er.at[e_slot], lsem.at[0])
        own.start()
        own.wait()
        wait_bytes(er.at[0 : NSEQ - 1], e_recv)

    @pl.when(jnp.logical_not(same))
    def _():
        send_piece(0, 0)
        wait_bytes(er, e_recv)

    pieces = jnp.sum(er[...].astype(F32).reshape(8, NSP, PAD, HD), axis=1)
    rests = tokens_of(pieces)
    for j in range(8):
        proj[:, j * COLS : j * COLS + HD] = pieces[j]
        proj[:, j * COLS + HD : (j + 1) * COLS] = rests[j, :, 0 : COLS - HD]
    updated = jnp.where(iota((PAD, FEAT), 0) < TOK, upd[...] + gate * proj[...], 0.0)
    hidden_out[...] = updated[0:TOK].astype(BF16)
    part = lax.dot_general(
        updated,
        headg_s[...],
        across,
        precision=lax.Precision.HIGHEST,
        preferred_element_type=F32,
    )
    part = jnp.where(iota((PAD, 64), 0) < TOK, part, fixed)
    gs[...] = jnp.zeros(gs.shape, F32)
    gs[:, 0:64] = part
    gs[:, 64:65] = jnp.sum(updated, axis=1, keepdims=True)
    gs[:, 65:66] = jnp.sum(updated * updated, axis=1, keepdims=True)

    def share(fn):
        for ds in (-1, 0, 1):
            for dp in range(NSP):
                if ds == 0 and dp == 0:
                    continue
                inside = jnp.logical_and(s + ds >= 0, s + ds < NSEQ)
                pl.when(inside)(functools.partial(fn, ds, dp))

    def g_start(ds, dp):
        pltpu.make_async_remote_copy(
            src_ref=gs,
            dst_ref=gr.at[(1 - ds) * NSP + dp],
            send_sem=g_send.at[(ds + 1) * NSP + dp],
            recv_sem=g_recv.at[(1 - ds) * NSP + dp],
            device_id=(s + ds, lax.rem(p + dp, NSP)),
            device_id_type=MESH,
        ).start()

    def g_wait(ds, dp):
        slot = (ds + 1) * NSP + dp
        wait_bytes(gr.at[slot], g_recv.at[slot])
        wait_bytes(gr.at[slot], g_send.at[slot])

    share(g_start)
    gr[NSP] = gs[...]
    share(g_wait)

    vtok[...] = jnp.zeros(vtok.shape, F32)
    vcell[...] = jnp.zeros(vcell.shape, F32)
    for ds in (-1, 0, 1):
        inside = jnp.logical_and(s + ds >= 0, s + ds < NSEQ)
        total = gr[(ds + 1) * NSP]
        for dp in range(1, NSP):
            total = total + gr[(ds + 1) * NSP + dp]
        mean = total[0:TOK, 64:65] / D
        var = total[0:TOK, 65:66] / D - mean * mean
        scaled = (total[0:TOK, 0:64] - mean * total[12:13, 0:64]) * lax.rsqrt(var + 1e-6)
        velocity = scaled + total[13:14, 0:64] + headb_ref[...]
        vtok[ds + 1, 1 : TOK + 1, 0:64] = jnp.where(inside, velocity, 0.0)
        around = vtok[ds + 1, pl.ds(3 * p, 8), :]
        for a in range(2):
            for c2 in range(2):
                col = (a * 2 + c2) * 16
                vcell[2 * ds + 2 + a, pl.ds(c2, 8, stride=2), :] = around[:, col : col + 16]

    clean = cells[0] - NOISE * vcell[...]
    cells[0] = clean
    first = firsts[:, 0:8, :].reshape(32, VAE)
    for dy, dx in taps():
        first += jnp.dot(
            window(cells, 0, dy, dx, 4), win_s[18 + dy * 3 + dx], preferred_element_type=F32
        )
    norm = lax.rsqrt(jnp.mean(first * first, axis=-1, keepdims=True) + 1e-6)
    z = first * norm * row_of(vgain_ref, 0, 3)
    act = z / (1.0 + jnp.exp(-z))
    pos = iota((32, VAE), 0)
    y = 2 * s - 1 + pos // 8
    x = 6 * p - 1 + pos % 8
    inside = (y >= 0) & (y < 2 * NSEQ) & (x >= 0) & (x < 24)
    act = jnp.where(inside, act, 0.0)
    firsts[:, 0:8, :] = first.reshape(4, 8, VAE)
    acts[...] = jnp.zeros(acts.shape, F32)
    acts[0, :, 0:8, :] = act.reshape(4, 8, VAE)
    out = mid + firsts[1:3, 1:9, :].reshape(16, VAE)
    for dy, dx in taps():
        out += jnp.dot(
            window(acts, 0, dy, dx, 2), wmid_s[18 + dy * 3 + dx], preferred_element_type=F32
        )
    out = out.reshape(2, 8, VAE)
    for x in range(6):
        decoded_out[x] = out[:, x, :]

    wait_all(qd, q2_send.at[0])
    for c in range(CH):
        wait_all(rc.at[c], c_send.at[c])
        if c > 0:
            wait_plane(c, qp, q1_send)
            wait_line(c, ql, q2_send)
        if c < LAST:
            wait_plane(c, agp, d1_send)
            wait_line(c, agl, d2_send)
    wait_all(ag, d2_send.at[LAST])

    @pl.when(same)
    def _():
        wait_bytes(er.at[0 : NSEQ - 1], e_send)

    @pl.when(jnp.logical_not(same))
    def _():
        wait_bytes(er, e_send)


def hand_out(hidden_ref, decoded_ref, hidden_out, decoded_out):
    hidden_out[...] = hidden_ref[...]
    decoded_out[...] = decoded_ref[...]


def local(
    group_hidden,
    queries,
    history_keys,
    history_values,
    valid_len,
    out_weight,
    attn_gate,
    head_gain,
    head_shift,
    head_weight,
    head_bias,
    noisy_latent,
    prev_latent,
    prev_feat,
    conv_in_weight,
    conv_in_bias,
    vae_gain,
    conv_mid_weight,
    conv_mid_bias,
):
    vmem = pl.BlockSpec(memory_space=pltpu.VMEM)
    hbm = pl.BlockSpec(memory_space=pl.ANY)
    smem = pl.BlockSpec(memory_space=pltpu.SMEM)
    dma = pltpu.SemaphoreType.DMA
    hidden, decoded = pl.pallas_call(
        kernel,
        out_shape=(
            jax.ShapeDtypeStruct((TOK, FEAT), BF16),
            jax.ShapeDtypeStruct((6, 2, VAE), F32),
        ),
        in_specs=[vmem, vmem, hbm, hbm, smem, hbm] + [vmem] * 7 + [hbm, vmem, vmem, vmem, hbm, hbm],
        out_specs=(vmem, vmem),
        scratch_shapes=[
            pltpu.VMEM((CH, HIST, CW), BF16),
            pltpu.VMEM((CH, HIST, CW), BF16),
            pltpu.VMEM((COLS, FEAT), BF16),
            pltpu.VMEM((64, FEAT), F32),
            pltpu.VMEM((64, FEAT), F32),
            pltpu.VMEM((27, 16, VAE), BF16),
            pltpu.VMEM((27, VAE, VAE), BF16),
            pltpu.VMEM((CH, PAD, CW), BF16),
            pltpu.VMEM((NSEQ, PAD, CW), BF16),
            pltpu.VMEM((CH, PLANE, PAD, CW), BF16),
            pltpu.VMEM((CH, LINE, ROWS, CW), BF16),
            pltpu.VMEM((CH, PAD, CW), BF16),
            pltpu.VMEM((CH, PLANE, PAD, CW), BF16),
            pltpu.VMEM((CH, LINE, ROWS, CW), BF16),
            pltpu.VMEM((CH, NSEQ, PAD, CW), BF16),
            pltpu.VMEM((CH, NSEQ, PAD, CW), BF16),
            pltpu.VMEM((NSEQ, PAD, CW), BF16),
            pltpu.VMEM((NSEQ, PAD, HD), BF16),
            pltpu.VMEM((NSEQ, PAD, HD), BF16),
            pltpu.VMEM((PAD, HD), F32),
            pltpu.VMEM((3 * NSP, PAD, HD), F32),
            pltpu.VMEM((2, 8, HD), F32),
            pltpu.VMEM((9, 2, 8, HD), F32),
            pltpu.VMEM((2, 16, VAE), BF16),
            pltpu.VMEM((9, 2, 16, VAE), BF16),
            pltpu.VMEM((4, 8, VAE), F32),
            pltpu.VMEM((3, 6, 16, 16), F32),
            pltpu.VMEM((3, 24, HD), F32),
            pltpu.VMEM((6, 16, 16), F32),
            pltpu.VMEM((2, 4, 16, VAE), F32),
            pltpu.VMEM((4, 16, VAE), F32),
            pltpu.VMEM((1, 4, 16, VAE), F32),
            pltpu.VMEM((PAD, FEAT), F32),
            pltpu.VMEM((PAD, FEAT), F32),
            dma((CH,)),
            dma((CH,)),
            dma((4,)),
            dma((1,)),
        ]
        + [dma((CH,))] * 10
        + [
            dma,
            dma,
            dma((3 * NSP,)),
            dma((3 * NSP,)),
            dma((9,)),
            dma((9,)),
            dma((9,)),
            dma((9,)),
        ],
        compiler_params=pltpu.CompilerParams(
            collective_id=0, has_side_effects=True, vmem_limit_bytes=56 << 20
        ),
    )(
        group_hidden,
        queries,
        history_keys,
        history_values,
        valid_len,
        out_weight.T,
        attn_gate.reshape(-1, HD),
        head_gain.reshape(-1, HD),
        head_shift.reshape(-1, HD),
        head_bias.reshape(1, -1),
        conv_in_bias.reshape(-1, HD),
        vae_gain.reshape(-1, HD),
        conv_mid_bias.reshape(-1, HD),
        head_weight.T,
        noisy_latent.transpose(1, 0, 2),
        prev_latent.transpose(0, 2, 1, 3),
        prev_feat.transpose(0, 2, 1, 3),
        conv_in_weight.reshape(27, 16, VAE),
        conv_mid_weight.reshape(27, VAE, VAE),
    )
    hidden, decoded = pl.pallas_call(
        hand_out,
        out_shape=(
            jax.ShapeDtypeStruct((TOK, FEAT), BF16),
            jax.ShapeDtypeStruct((6, 2, VAE), F32),
        ),
        in_specs=[vmem, vmem],
        out_specs=(vmem, vmem),
    )(hidden, decoded)
    return hidden, decoded.transpose(1, 0, 2)


def solution(mesh):
    placed = (
        P("seq", "sp"),
        P("seq", "sp"),
        P("seq", "sp"),
        P("seq", "sp"),
        P("seq"),
        P("sp", "seq"),
        P("sp"),
        P(),
        P(),
        P(),
        P(),
        P("seq", "sp", None),
        P(None, "seq", "sp", None),
        P(None, "seq", "sp", None),
        P(),
        P(),
        P(),
        P(),
        P(),
    )
    return jax.shard_map(
        local,
        mesh=mesh,
        in_specs=placed,
        out_specs=(P("seq", "sp"), P("seq", "sp", None)),
        check_vma=False,
    )
```

```python
import functools
import math

import jax
import jax.numpy as jnp
from jax import lax
from jax.experimental import pallas as pl
from jax.experimental.pallas import tpu as pltpu
from jax.sharding import PartitionSpec as P

MESH = pl.DeviceIdType.MESH
BF16 = jnp.bfloat16
F32 = jnp.float32

D = 5120
HD = 128
NSEQ = 32
NSP = 4
TOK = 12
PAD = 16
TOKENS = NSEQ * TOK
HIST = 2048
FEAT = 1280
COLS = 160
CH = 5
CW = FEAT // CH
LINE = 4
PLANE = NSEQ // LINE
ROWS = PLANE * TOK
BY_Y = (False, True, False, True, False)
LAST = CH - 1
VAE = 384
EXP2_SCALE = math.log2(math.e) / math.sqrt(HD)
NOISE = 0.75


def iota(shape, dim):
    return lax.broadcasted_iota(jnp.int32, shape, dim)


def row_of(ref, start, count):
    return jnp.concatenate([ref[pl.ds(start + k, 1), :] for k in range(count)], axis=1)


def wait_bytes(region, sem):
    pltpu.make_async_copy(region, region, sem).wait()


def pad_rows(rows):
    width = rows.shape[-1]
    pairs = rows.reshape(-1, 2 * TOK, width)
    even = pairs[:, :PAD]
    odd = pltpu.roll(pairs, TOK, 1)[:, :PAD]
    return jnp.concatenate([even[:, None], odd[:, None]], axis=1).reshape(-1, PAD, width)


def pack_rows(blocks):
    width = blocks.shape[-1]
    pairs = blocks.reshape(-1, 2, PAD, width)
    zeros = jnp.zeros((pairs.shape[0], 8, width), F32)
    even = jnp.concatenate([pairs[:, 0], zeros], axis=1)
    odd = pltpu.roll(jnp.concatenate([pairs[:, 1], zeros], axis=1), TOK, 1)
    row = iota(even.shape, 1)
    return jnp.where(row < TOK, even, odd).reshape(-1, width)


def kernel(
    hidden_ref,
    q_ref,
    k_hbm,
    v_hbm,
    valid_ref,
    w_hbm,
    gate_ref,
    gain_ref,
    shift_ref,
    headb_ref,
    bias_in_ref,
    vgain_ref,
    bias_mid_ref,
    headw_hbm,
    noisy_ref,
    platent_ref,
    pfeat_ref,
    win_hbm,
    wmid_hbm,
    hidden_out,
    decoded_out,
    k_s,
    v_s,
    w_s,
    headw_s,
    headg_s,
    win_s,
    wmid_s,
    qs,
    qd,
    qp,
    ql,
    ao,
    agp,
    agl,
    pc,
    rc,
    ag,
    es,
    er,
    gs,
    gr,
    ls,
    lr,
    fs,
    fr,
    fpad,
    cells,
    vtok,
    vcell,
    feats,
    firsts,
    acts,
    proj,
    upd,
    ksem,
    vsem,
    wsem,
    lsem,
    q1_send,
    q1_recv,
    q2_send,
    q2_recv,
    d1_send,
    d1_recv,
    d2_send,
    d2_recv,
    c_send,
    c_recv,
    e_send,
    e_recv,
    g_send,
    g_recv,
    l_send,
    l_recv,
    f_send,
    f_recv,
    ready,
):
    s = lax.axis_index("seq")
    p = lax.axis_index("sp")
    owner_sp = s // 8
    piece = lax.rem(s, 8)

    barrier = pltpu.get_barrier_semaphore()

    def greet(to_s, to_p):
        pl.semaphore_signal(barrier, inc=1, device_id=(to_s, to_p), device_id_type=MESH)

    def greet_seq(k, _):
        greet(lax.rem(s + k, NSEQ), p)
        return 0

    lax.fori_loop(1, NSEQ, greet_seq, 0)

    for dp in (1, 2, 3):
        greet(s, lax.rem(p + dp, NSP))

    loads = []
    for c in range(CH):
        cols = pl.ds(c * CW, CW)
        kc = pltpu.make_async_copy(k_hbm.at[:, cols], k_s.at[c], ksem.at[c])
        vc = pltpu.make_async_copy(v_hbm.at[:, cols], v_s.at[c], vsem.at[c])
        kc.start()
        vc.start()
        loads.append((kc, vc))
    w_copy = pltpu.make_async_copy(w_hbm, w_s, wsem.at[0])
    head_cols = pl.ds(pl.multiple_of(p * FEAT, FEAT), FEAT)
    head_copy = pltpu.make_async_copy(headw_hbm.at[:, head_cols], headw_s, wsem.at[1])
    win_copy = pltpu.make_async_copy(win_hbm, win_s, wsem.at[2])
    wmid_copy = pltpu.make_async_copy(wmid_hbm, wmid_s, wsem.at[3])
    for copy in (win_copy, wmid_copy, w_copy, head_copy):
        copy.start()

    qs[...] = jnp.zeros(qs.shape, BF16)
    for c in range(CH):
        qs[c, 0:TOK, :] = q_ref[:, c * CW : (c + 1) * CW]
    x_at, y_at, z_at = s // 8, lax.rem(s // 2, 4), lax.rem(s, 2)

    def line_at(c):
        return y_at if BY_Y[c] else x_at

    def plane_at(c):
        return x_at * 2 + z_at if BY_Y[c] else y_at * 2 + z_at

    def line_peer(c, line):
        return x_at * 8 + line * 2 + z_at if BY_Y[c] else line * 8 + y_at * 2 + z_at

    def plane_peer(c, at):
        return (at // 2) * 8 + y_at * 2 + lax.rem(at, 2) if BY_Y[c] else x_at * 8 + at

    def to_line(c, buf, dst, send_sem, recv_sem, by_dest):
        for k in range(1, LINE):
            line = lax.rem(line_at(c) + k, LINE)
            pltpu.make_async_remote_copy(
                src_ref=buf.at[c, line if by_dest else line_at(c)],
                dst_ref=dst.at[c, line_at(c)],
                send_sem=send_sem.at[c],
                recv_sem=recv_sem.at[c],
                device_id=(line_peer(c, line), p),
                device_id_type=MESH,
            ).start()

    def to_plane(c, buf, dst, send_sem, recv_sem, by_dest):
        for k in range(1, PLANE):
            at = lax.rem(plane_at(c) + k, PLANE)
            pltpu.make_async_remote_copy(
                src_ref=buf.at[c, at] if by_dest else buf.at[c],
                dst_ref=dst.at[c, plane_at(c)],
                send_sem=send_sem.at[c],
                recv_sem=recv_sem.at[c],
                device_id=(plane_peer(c, at), p),
                device_id_type=MESH,
            ).start()

    def wait_line(c, dst, sem):
        wait_bytes(dst.at[c, 0 : LINE - 1], sem.at[c])

    def wait_plane(c, dst, sem):
        wait_bytes(dst.at[c, 0 : PLANE - 1], sem.at[c])

    ls[...] = jnp.zeros(ls.shape, F32)
    for x in range(6):
        ls[:, x, 0:16] = noisy_ref[x]
        ls[:, x, 16:32] = platent_ref[0, x].astype(F32)
        ls[:, x, 32:48] = platent_ref[1, x].astype(F32)
    fpad[...] = jnp.zeros(fpad.shape, F32)
    for f in range(2):
        for x in range(6):
            for r in range(2):
                fpad[2 * r + f, x, :] = pfeat_ref[f, x, r].astype(F32)
    fs[...] = fpad[...].reshape(2, 2 * 8, VAE).astype(BF16)

    pl.semaphore_wait(barrier, NSEQ - 1 + 3)
    for dp in (1, 2, 3):
        pl.semaphore_signal(
            ready, inc=1, device_id=(s, lax.rem(p + dp, NSP)), device_id_type=MESH
        )

    def place(c, owner):
        if not BY_Y[c]:
            return owner
        return lax.rem(owner // 2, 4) * 8 + (owner // 8) * 2 + lax.rem(owner, 2)

    def to_all(src, dst, send_sem, recv_sem):
        def one(k, _):
            to = lax.rem(s + k, NSEQ)
            pltpu.make_async_remote_copy(
                src_ref=src(to),
                dst_ref=dst,
                send_sem=send_sem,
                recv_sem=recv_sem,
                device_id=(to, p),
                device_id_type=MESH,
            ).start()
            return 0

        lax.fori_loop(1, NSEQ, one, 0)

    def wait_all(dst, sem):
        wait_bytes(dst.at[0 : NSEQ - 1], sem)

    to_all(lambda to: qs.at[0], qd.at[s], q2_send.at[0], q2_recv.at[0])
    for c in range(1, CH):
        to_plane(c, qs, qp, q1_send, q1_recv, False)
    qd[pl.ds(s, 1)] = qs[0][None]

    def near(fn):
        for ds in (-1, 0, 1):
            for dp in (-1, 0, 1):
                if ds == 0 and dp == 0:
                    continue
                inside_s = jnp.logical_and(s + ds >= 0, s + ds < NSEQ)
                inside_p = jnp.logical_and(p + dp >= 0, p + dp < NSP)
                pl.when(jnp.logical_and(inside_s, inside_p))(functools.partial(fn, ds, dp))

    def slot_of(ds, dp):
        return (ds + 1) * 3 + dp + 1

    def border_copies(ds, dp):
        out, back = slot_of(ds, dp), slot_of(-ds, -dp)
        rows = {-1: slice(0, 1), 0: slice(0, 2), 1: slice(1, 2)}[ds]
        return [
            pltpu.make_async_remote_copy(
                src_ref=src,
                dst_ref=dst,
                send_sem=send.at[out],
                recv_sem=recv.at[back],
                device_id=(s + ds, p + dp),
                device_id_type=MESH,
            )
            for src, dst, send, recv in (
                (ls, lr.at[back], l_send, l_recv),
                (fs.at[rows], fr.at[back, rows], f_send, f_recv),
            )
        ]

    def border_start(ds, dp):
        for copy in border_copies(ds, dp):
            copy.start()

    def border_wait(ds, dp):
        slot = slot_of(ds, dp)
        part = fr.at[slot, 0:1] if ds else fr.at[slot]
        wait_bytes(lr.at[slot], l_recv.at[slot])
        wait_bytes(part, f_recv.at[slot])

    def border_left(ds, dp):
        slot = slot_of(ds, dp)
        part = fr.at[slot, 0:1] if ds else fr.at[slot]
        wait_bytes(lr.at[slot], l_send.at[slot])
        wait_bytes(part, f_send.at[slot])


    visible = iota((1, HIST), 1) < valid_ref[0]
    ones = jnp.ones((HIST, HD), BF16)
    half = TOKENS // 2
    lane = iota((half, HD), 1) % 32
    across = (((1,), (1,)), ((), ()))

    def spread_queries(c):
        qp[c, pl.ds(plane_at(c), 1)] = qs[c][None]
        wait_plane(c, qp, q1_recv)
        ql[c, pl.ds(line_at(c), 1)] = pack_rows(qp[c].astype(F32)).astype(BF16)[None]
        to_line(c, ql, ql, q2_send, q2_recv, False)

    def attend_ready(c):
        if c == 0:
            wait_all(qd, q2_recv.at[0])
        else:
            wait_line(c, ql, q2_recv)
        loads[c][0].wait()
        loads[c][1].wait()

    def spare_rows(st):
        at = iota(st.shape, 2)
        return jnp.where(
            at < 32,
            pltpu.roll(st, 12, 1),
            jnp.where(at < 64, pltpu.roll(st, 8, 1), pltpu.roll(st, 4, 1)),
        )

    def tokens_of(tile):
        at = iota(tile.shape, 1)
        return jnp.where(
            at < 4,
            pltpu.roll(tile, 4, 1),
            jnp.where(
                at < 8,
                pltpu.roll(pltpu.roll(tile, HD - 32, 2), 8, 1),
                pltpu.roll(pltpu.roll(tile, HD - 64, 2), 12, 1),
            ),
        )

    def attend(c):
        for r in range(2):
            owners = slice(r * (NSEQ // 2), (r + 1) * (NSEQ // 2))
            if c == 0:
                q = pack_rows(qd[owners].astype(F32)).astype(BF16)
            else:
                q = ql[c, 2 * r : 2 * r + 2].reshape(half, CW)
            stats = jnp.zeros((half, HD), F32)
            for h in range(2):
                cols = slice(h * HD, (h + 1) * HD)
                scores = lax.dot_general(
                    q[:, cols], k_s[c, :, cols], across, preferred_element_type=F32
                )
                scores = jnp.where(visible, scores, -1e30)
                top = jnp.max(scores, axis=1, keepdims=True) * EXP2_SCALE
                top = top.astype(BF16).astype(F32)
                weights = jnp.exp2(scores * EXP2_SCALE - top).astype(BF16)
                both = jnp.concatenate([v_s[c, :, cols], ones], axis=1)
                acc = jnp.dot(weights, both, preferred_element_type=F32)
                total = acc[:, HD:]
                high = total.astype(BF16).astype(F32)
                stats = jnp.where(lane == h, top, stats)
                stats = jnp.where(lane == 2 + h, high, stats)
                stats = jnp.where(lane == 4 + h, total - high, stats)
                tile = pad_rows(acc[:, :HD])
                if h == 1:
                    tile = jnp.where(iota(tile.shape, 1) < TOK, tile, spare_rows(pad_rows(stats)))
                pc[c, owners, :, cols] = tile.astype(BF16)

    def send_partials(c):
        rc[c, pl.ds(s, 1)] = pc[c, pl.ds(place(c, s), 1)]
        to_all(lambda to: pc.at[c, place(c, to)], rc.at[c, s], c_send.at[c], c_recv.at[c])

    def merge_owned(c, parts):
        st = tokens_of(parts[:, :, HD : 2 * HD].astype(F32))
        top = jnp.max(st, axis=0, keepdims=True)
        factor = jnp.exp2(st - top)
        sums = pltpu.roll(st, HD - 2, 2) + pltpu.roll(st, HD - 4, 2)
        factor = factor / jnp.sum(factor * sums, axis=0, keepdims=True)
        row = iota((PAD, HD), 0)
        for h in range(2):
            part = parts[:, :, h * HD : (h + 1) * HD].astype(F32)
            merged = jnp.sum(part * factor[:, :, h : h + 1], axis=0)
            merged = jnp.where(row < TOK, merged, 0.0)
            ao[c, :, h * HD : (h + 1) * HD] = merged.astype(BF16)

    def spread_attention(c):
        wait_plane(c, agp, d1_recv)
        agl[c, pl.ds(line_at(c), 1)] = pack_rows(agp[c].astype(F32)).astype(BF16)[None]
        to_line(c, agl, agl, d2_send, d2_recv, False)

    def merge(c):
        merge_owned(c, rc[c])
        if c == LAST:
            ag[pl.ds(s, 1)] = ao[c][None]
        else:
            agp[c, pl.ds(plane_at(c), 1)] = ao[c][None]

    def send_attention(c):
        if c == LAST:
            to_all(lambda to: ao.at[c], ag.at[s], d2_send.at[c], d2_recv.at[c])
        else:
            to_plane(c, ao, agp, d1_send, d1_recv, False)

    for c in range(1, CH):
        spread_queries(c)
    pl.semaphore_wait(ready, 3)
    near(border_start)
    for c in range(CH):
        attend_ready(c)
        if c >= 3:
            wait_all(rc.at[c - 3], c_recv.at[c - 3])
        attend(c)
        if c >= 3:
            merge(c - 3)
        send_partials(c)
        if c >= 3:
            send_attention(c - 3)
    spread_attention(0)

    near(border_wait)
    win_copy.wait()
    wmid_copy.wait()
    lr[4] = ls[...]
    fr[4] = fs[...]
    cells[...] = jnp.zeros(cells.shape, F32)
    feats[...] = jnp.zeros(feats.shape, F32)
    for ds in (-1, 0, 1):
        for dp in (-1, 0, 1):
            inside = jnp.logical_and(
                jnp.logical_and(s + ds >= 0, s + ds < NSEQ),
                jnp.logical_and(p + dp >= 0, p + dp < NSP),
            )
            slot = slot_of(ds, dp)
            src = {-1: slice(4, 6), 0: slice(0, 6), 1: slice(0, 2)}[dp]
            dst = {-1: slice(0, 2), 0: slice(2, 8), 1: slice(8, 10)}[dp]
            for g in range(3):
                part = lr[slot, :, src, g * 16 : (g + 1) * 16]
                cells[g, 2 * ds + 2 : 2 * ds + 4, dst, :] = jnp.where(inside, part, 0.0)
            src = {-1: slice(5, 6), 0: slice(0, 6), 1: slice(0, 1)}[dp]
            dst = {-1: slice(0, 1), 0: slice(1, 7), 1: slice(7, 8)}[dp]
            part = fr[slot].astype(F32).reshape(2, 2, 8, VAE)
            part = jnp.where(inside, part, 0.0)
            rows = {-1: (1,), 0: (0, 1), 1: (0,)}[ds]
            for row in rows:
                for f in range(2):
                    feats[f, {-1: 0, 0: 1 + row, 1: 3}[ds], dst, :] = part[row, f, src, :]

    def window(ref, g, dy, dx, height):
        return ref[g, dy : dy + height, dx : dx + 8, :].reshape(height * 8, -1).astype(BF16)

    def taps():
        return [(dy, dx) for dy in range(3) for dx in range(3)]

    first = jnp.zeros((32, VAE), F32) + row_of(bias_in_ref, 0, 3)
    mid = jnp.zeros((16, VAE), F32) + row_of(bias_mid_ref, 0, 3)
    for f in range(2):
        for dy, dx in taps():
            tap = f * 9 + dy * 3 + dx
            first += jnp.dot(window(cells, f + 1, dy, dx, 4), win_s[tap], preferred_element_type=F32)
            mid += jnp.dot(window(feats, f, dy, dx, 2), wmid_s[tap], preferred_element_type=F32)
    firsts[:, 0:8, :] = first.reshape(4, 8, VAE)

    def merge_and_send(c):
        wait_all(rc.at[c], c_recv.at[c])
        merge(c)
        send_attention(c)

    merge_and_send(2)
    spread_attention(1)
    merge_and_send(3)
    spread_attention(2)

    gate, gain = row_of(gate_ref, 0, 10), row_of(gain_ref, 10 * p, 10)
    shift = row_of(shift_ref, 10 * p, 10)
    head_copy.wait()
    headg_s[...] = headw_s[...] * gain
    fixed = lax.dot_general(
        jnp.where(iota((PAD, FEAT), 0) == TOK, gain, shift),
        headw_s[...],
        across,
        precision=lax.Precision.HIGHEST,
        preferred_element_type=F32,
    )
    upd[...] = jnp.zeros(upd.shape, F32)
    upd[0:TOK, :] = hidden_ref[...].astype(F32)

    spread_attention(3)
    merge_and_send(LAST)

    w_copy.wait()

    def agl_ready(c):
        wait_line(c, agl, d2_recv)
        return agl[c].reshape(TOKENS, CW)

    def project(c, block):
        cols = w_s[:, c * CW : (c + 1) * CW]
        return lax.dot_general(block, cols, across, preferred_element_type=F32)

    by_x = pad_rows(project(0, agl_ready(0)) + project(2, agl_ready(2)))
    by_y = project(1, agl_ready(1))
    by_y = pad_rows(by_y + project(3, agl_ready(3))).reshape(4, 4, 2, PAD, COLS)
    result = by_x + jnp.stack([by_y[:, x] for x in range(4)]).reshape(NSEQ, PAD, COLS)
    wait_all(ag, d2_recv.at[LAST])
    result += project(LAST, ag[...].reshape(NSEQ * PAD, CW)).reshape(NSEQ, PAD, COLS)
    rest = jnp.concatenate([result[:, :, HD:], jnp.zeros((NSEQ, PAD, 2 * HD - COLS), F32)], axis=2)
    rest = rest + pltpu.roll(rest, 32, 2) + pltpu.roll(rest, 64, 2)
    tile = jnp.where(iota(rest.shape, 1) < TOK, result[:, :, :HD], spare_rows(rest))
    es[...] = tile.astype(BF16)
    e_slot = piece * NSP + p
    same = owner_sp == p

    def send_piece(k, _):
        to = lax.rem(s + k, NSEQ)
        pltpu.make_async_remote_copy(
            src_ref=es.at[to],
            dst_ref=er.at[e_slot],
            send_sem=e_send,
            recv_sem=e_recv,
            device_id=(to, owner_sp),
            device_id_type=MESH,
        ).start()
        return 0

    lax.fori_loop(1, NSEQ, send_piece, 0)

    @pl.when(same)
    def _():
        own = pltpu.make_async_copy(es.at[s], er.at[e_slot], lsem.at[0])
        own.start()
        own.wait()
        wait_bytes(er.at[0 : NSEQ - 1], e_recv)

    @pl.when(jnp.logical_not(same))
    def _():
        send_piece(0, 0)
        wait_bytes(er, e_recv)

    pieces = jnp.sum(er[...].astype(F32).reshape(8, NSP, PAD, HD), axis=1)
    rests = tokens_of(pieces)
    for j in range(8):
        proj[:, j * COLS : j * COLS + HD] = pieces[j]
        proj[:, j * COLS + HD : (j + 1) * COLS] = rests[j, :, 0 : COLS - HD]
    updated = jnp.where(iota((PAD, FEAT), 0) < TOK, upd[...] + gate * proj[...], 0.0)
    hidden_out[...] = updated[0:TOK].astype(BF16)
    part = lax.dot_general(
        updated,
        headg_s[...],
        across,
        precision=lax.Precision.HIGHEST,
        preferred_element_type=F32,
    )
    part = jnp.where(iota((PAD, 64), 0) < TOK, part, fixed)
    gs[...] = jnp.zeros(gs.shape, F32)
    gs[:, 0:64] = part
    gs[:, 64:65] = jnp.sum(updated, axis=1, keepdims=True)
    gs[:, 65:66] = jnp.sum(updated * updated, axis=1, keepdims=True)

    def share(fn):
        for ds in (-1, 0, 1):
            for dp in range(NSP):
                if ds == 0 and dp == 0:
                    continue
                inside = jnp.logical_and(s + ds >= 0, s + ds < NSEQ)
                pl.when(inside)(functools.partial(fn, ds, dp))

    def g_start(ds, dp):
        pltpu.make_async_remote_copy(
            src_ref=gs,
            dst_ref=gr.at[(1 - ds) * NSP + dp],
            send_sem=g_send.at[(ds + 1) * NSP + dp],
            recv_sem=g_recv.at[(1 - ds) * NSP + dp],
            device_id=(s + ds, lax.rem(p + dp, NSP)),
            device_id_type=MESH,
        ).start()

    def g_wait(ds, dp):
        slot = (ds + 1) * NSP + dp
        wait_bytes(gr.at[slot], g_recv.at[slot])

    def g_left(ds, dp):
        slot = (ds + 1) * NSP + dp
        wait_bytes(gr.at[slot], g_send.at[slot])

    share(g_start)
    gr[NSP] = gs[...]
    share(g_wait)

    vtok[...] = jnp.zeros(vtok.shape, F32)
    vcell[...] = jnp.zeros(vcell.shape, F32)
    for ds in (-1, 0, 1):
        inside = jnp.logical_and(s + ds >= 0, s + ds < NSEQ)
        total = gr[(ds + 1) * NSP]
        for dp in range(1, NSP):
            total = total + gr[(ds + 1) * NSP + dp]
        mean = total[0:TOK, 64:65] / D
        var = total[0:TOK, 65:66] / D - mean * mean
        scaled = (total[0:TOK, 0:64] - mean * total[12:13, 0:64]) * lax.rsqrt(var + 1e-6)
        velocity = scaled + total[13:14, 0:64] + headb_ref[...]
        vtok[ds + 1, 1 : TOK + 1, 0:64] = jnp.where(inside, velocity, 0.0)
        around = vtok[ds + 1, pl.ds(3 * p, 8), :]
        for a in range(2):
            for c2 in range(2):
                col = (a * 2 + c2) * 16
                vcell[2 * ds + 2 + a, pl.ds(c2, 8, stride=2), :] = around[:, col : col + 16]

    clean = cells[0] - NOISE * vcell[...]
    cells[0] = clean
    first = firsts[:, 0:8, :].reshape(32, VAE)
    for dy, dx in taps():
        first += jnp.dot(
            window(cells, 0, dy, dx, 4), win_s[18 + dy * 3 + dx], preferred_element_type=F32
        )
    norm = lax.rsqrt(jnp.mean(first * first, axis=-1, keepdims=True) + 1e-6)
    z = first * norm * row_of(vgain_ref, 0, 3)
    act = z / (1.0 + jnp.exp(-z))
    pos = iota((32, VAE), 0)
    y = 2 * s - 1 + pos // 8
    x = 6 * p - 1 + pos % 8
    inside = (y >= 0) & (y < 2 * NSEQ) & (x >= 0) & (x < 24)
    act = jnp.where(inside, act, 0.0)
    firsts[:, 0:8, :] = first.reshape(4, 8, VAE)
    acts[...] = jnp.zeros(acts.shape, F32)
    acts[0, :, 0:8, :] = act.reshape(4, 8, VAE)
    out = mid + firsts[1:3, 1:9, :].reshape(16, VAE)
    for dy, dx in taps():
        out += jnp.dot(
            window(acts, 0, dy, dx, 2), wmid_s[18 + dy * 3 + dx], preferred_element_type=F32
        )
    out = out.reshape(2, 8, VAE)
    for x in range(6):
        decoded_out[x] = out[:, x, :]

    near(border_left)
    share(g_left)
    wait_all(qd, q2_send.at[0])
    for c in range(CH):
        wait_all(rc.at[c], c_send.at[c])
        if c > 0:
            wait_plane(c, qp, q1_send)
            wait_line(c, ql, q2_send)
        if c < LAST:
            wait_plane(c, agp, d1_send)
            wait_line(c, agl, d2_send)
    wait_all(ag, d2_send.at[LAST])

    @pl.when(same)
    def _():
        wait_bytes(er.at[0 : NSEQ - 1], e_send)

    @pl.when(jnp.logical_not(same))
    def _():
        wait_bytes(er, e_send)


def hand_out(hidden_ref, decoded_ref, hidden_out, decoded_out):
    hidden_out[...] = hidden_ref[...]
    decoded_out[...] = decoded_ref[...]


def local(
    group_hidden,
    queries,
    history_keys,
    history_values,
    valid_len,
    out_weight,
    attn_gate,
    head_gain,
    head_shift,
    head_weight,
    head_bias,
    noisy_latent,
    prev_latent,
    prev_feat,
    conv_in_weight,
    conv_in_bias,
    vae_gain,
    conv_mid_weight,
    conv_mid_bias,
):
    vmem = pl.BlockSpec(memory_space=pltpu.VMEM)
    hbm = pl.BlockSpec(memory_space=pl.ANY)
    smem = pl.BlockSpec(memory_space=pltpu.SMEM)
    dma = pltpu.SemaphoreType.DMA
    hidden, decoded = pl.pallas_call(
        kernel,
        out_shape=(
            jax.ShapeDtypeStruct((TOK, FEAT), BF16),
            jax.ShapeDtypeStruct((6, 2, VAE), F32),
        ),
        in_specs=[vmem, vmem, hbm, hbm, smem, hbm] + [vmem] * 7 + [hbm, vmem, vmem, vmem, hbm, hbm],
        out_specs=(vmem, vmem),
        scratch_shapes=[
            pltpu.VMEM((CH, HIST, CW), BF16),
            pltpu.VMEM((CH, HIST, CW), BF16),
            pltpu.VMEM((COLS, FEAT), BF16),
            pltpu.VMEM((64, FEAT), F32),
            pltpu.VMEM((64, FEAT), F32),
            pltpu.VMEM((27, 16, VAE), BF16),
            pltpu.VMEM((27, VAE, VAE), BF16),
            pltpu.VMEM((CH, PAD, CW), BF16),
            pltpu.VMEM((NSEQ, PAD, CW), BF16),
            pltpu.VMEM((CH, PLANE, PAD, CW), BF16),
            pltpu.VMEM((CH, LINE, ROWS, CW), BF16),
            pltpu.VMEM((CH, PAD, CW), BF16),
            pltpu.VMEM((CH, PLANE, PAD, CW), BF16),
            pltpu.VMEM((CH, LINE, ROWS, CW), BF16),
            pltpu.VMEM((CH, NSEQ, PAD, CW), BF16),
            pltpu.VMEM((CH, NSEQ, PAD, CW), BF16),
            pltpu.VMEM((NSEQ, PAD, CW), BF16),
            pltpu.VMEM((NSEQ, PAD, HD), BF16),
            pltpu.VMEM((NSEQ, PAD, HD), BF16),
            pltpu.VMEM((PAD, HD), F32),
            pltpu.VMEM((3 * NSP, PAD, HD), F32),
            pltpu.VMEM((2, 8, HD), F32),
            pltpu.VMEM((9, 2, 8, HD), F32),
            pltpu.VMEM((2, 16, VAE), BF16),
            pltpu.VMEM((9, 2, 16, VAE), BF16),
            pltpu.VMEM((4, 8, VAE), F32),
            pltpu.VMEM((3, 6, 16, 16), F32),
            pltpu.VMEM((3, 24, HD), F32),
            pltpu.VMEM((6, 16, 16), F32),
            pltpu.VMEM((2, 4, 16, VAE), F32),
            pltpu.VMEM((4, 16, VAE), F32),
            pltpu.VMEM((1, 4, 16, VAE), F32),
            pltpu.VMEM((PAD, FEAT), F32),
            pltpu.VMEM((PAD, FEAT), F32),
            dma((CH,)),
            dma((CH,)),
            dma((4,)),
            dma((1,)),
        ]
        + [dma((CH,))] * 10
        + [
            dma,
            dma,
            dma((3 * NSP,)),
            dma((3 * NSP,)),
            dma((9,)),
            dma((9,)),
            dma((9,)),
            dma((9,)),
            pltpu.SemaphoreType.REGULAR,
        ],
        compiler_params=pltpu.CompilerParams(
            collective_id=0, has_side_effects=True, vmem_limit_bytes=56 << 20
        ),
    )(
        group_hidden,
        queries,
        history_keys,
        history_values,
        valid_len,
        out_weight.T,
        attn_gate.reshape(-1, HD),
        head_gain.reshape(-1, HD),
        head_shift.reshape(-1, HD),
        head_bias.reshape(1, -1),
        conv_in_bias.reshape(-1, HD),
        vae_gain.reshape(-1, HD),
        conv_mid_bias.reshape(-1, HD),
        head_weight.T,
        noisy_latent.transpose(1, 0, 2),
        prev_latent.transpose(0, 2, 1, 3),
        prev_feat.transpose(0, 2, 1, 3),
        conv_in_weight.reshape(27, 16, VAE),
        conv_mid_weight.reshape(27, VAE, VAE),
    )
    hidden, decoded = pl.pallas_call(
        hand_out,
        out_shape=(
            jax.ShapeDtypeStruct((TOK, FEAT), BF16),
            jax.ShapeDtypeStruct((6, 2, VAE), F32),
        ),
        in_specs=[vmem, vmem],
        out_specs=(vmem, vmem),
    )(hidden, decoded)
    return hidden, decoded.transpose(1, 0, 2)


def solution(mesh):
    placed = (
        P("seq", "sp"),
        P("seq", "sp"),
        P("seq", "sp"),
        P("seq", "sp"),
        P("seq"),
        P("sp", "seq"),
        P("sp"),
        P(),
        P(),
        P(),
        P(),
        P("seq", "sp", None),
        P(None, "seq", "sp", None),
        P(None, "seq", "sp", None),
        P(),
        P(),
        P(),
        P(),
        P(),
    )
    return jax.shard_map(
        local,
        mesh=mesh,
        in_specs=placed,
        out_specs=(P("seq", "sp"), P("seq", "sp", None)),
        check_vma=False,
    )
```
